256 devices in a mesh: row: 16 (over x, y_hi, core), col: 16 (over z, y_lo).
Axes of the slice: x: 4, y: 4 (y_hi: 2, y_lo: 2; y = y_hi * 2 + y_lo), z: 8, core: 2. Of those that a mesh axis runs over, the one named last changes fastest.
Arguments:
- forward_fields: bfloat16 [4, 512, 512, 256], P(None, 'row', 'col'), may hold values from -6 to 6
- adjoint_now: float32 [512, 512, 256], P('row', 'col'), may hold values from -6 to 6
- adjoint_prev: float32 [512, 512, 256], P('row', 'col'), may hold values from -6 to 6
- courant_sq: float32 [512, 512, 256], P('row', 'col'), may hold values from 0.04 to 0.2
- receiver_cells: int32 [16, 16, 512], P('row', 'col'), may hold values from 0 to 262143
- traces: float32 [16, 16, 4, 512], P('row', 'col'), may hold values from -6 to 6
Outputs:
- smoothed: float32 [512, 512, 256], P('row', 'col')
- final_now: float32 [512, 512, 256], P('row', 'col')
- final_prev: float32 [512, 512, 256], P('row', 'col')
The draws below stay inside these ranges and needn't reach their ends.
All inputs are finite; a program needn't handle non-finite values.
Results may differ from the reference program's by a relative error of at most 0.0003.
Values sent between devices are 32-bit elements; how exact they have to be, the bound alone decides.
No kernel may reach another device: no remote copies, remote signals or barrier semaphores. Data moves between devices by JAX's collectives and lax.ppermute only.
A program may use at most 64 MiB of HBM per device.

```python
import math
import jax
import jax.numpy as jnp

CX = 32
CY = 32
NZ = 256
STEPS = 4
RECV = 512
KX = 128
KY = 128
KZ = 64
BRICKS_X = 16
BRICKS_Y = 16
NX = 512
NY = 512


def place_ends(drawn, stream_key, low, high):
    longest = drawn.shape.index(max(drawn.shape))
    spots = []
    for shift in (0, 1):
        where = [jax.random.randint(jax.random.fold_in(stream_key, axis), (), 0, length) for axis, length in enumerate(drawn.shape)]
        where[longest] = (where[longest] + shift) % drawn.shape[longest]
        spots.append(tuple(where))
    return drawn.at[spots[0]].set(low).at[spots[1]].set(high)


def block_levels(key, dims, pieces, smallest, high):
    gain = 1.0
    for dim, blocks in pieces:
        heights = jax.random.uniform(jax.random.fold_in(jax.random.fold_in(key, 6), dim), (blocks,), jnp.float32, smallest / len(pieces), high / len(pieces))
        gain = gain * jnp.repeat(jnp.exp(heights), dims[dim] // blocks).reshape((-1,) + (1,) * (len(dims) - 1 - dim))
    return gain


def normal_values(stream_key, extent, scale, limit, split=(), kind=jnp.bfloat16):
    gain = block_levels(stream_key, extent, split, -0.22, 0.18) if split else 1.0
    result = jax.random.normal(stream_key, extent, jnp.float32) * scale * gain
    return jnp.minimum(jnp.maximum(result, -limit), limit).astype(kind)


def setup_inputs(seed: int = 0) -> dict:
    splits = jax.random.split(jax.random.key(seed), 7)
    forward_fields = normal_values(splits[0], (STEPS, NX, NY, NZ), 1.0, 6.0, ((1, 16), (2, 16)))
    adjoint_now = normal_values(splits[1], (NX, NY, NZ), 1.0, 6.0, ((0, 16), (1, 16)), jnp.float32)
    adjoint_prev = normal_values(splits[2], (NX, NY, NZ), 1.0, 6.0, ((0, 16), (1, 16)), jnp.float32)
    courant_sq = jnp.clip(jnp.exp(math.log(0.2) - 1.609438 * jax.random.uniform(splits[3], (NX, NY, NZ), jnp.float32) ** block_levels(splits[3], (NX, NY, NZ), ((0, 16), (1, 16)), -0.2, 0.2)), 0.04, 0.2)
    receiver_cells = place_ends(jax.random.randint(splits[4], (BRICKS_X, BRICKS_Y, RECV), 0, CX * CY * NZ), jax.random.fold_in(splits[4], 1), 0, (CX * CY * NZ) - 1).astype(jnp.int32)
    traces = normal_values(splits[5], (BRICKS_X, BRICKS_Y, STEPS, RECV), 1.0, 6.0, ((0, 16), (1, 16)), jnp.float32)
    return dict(forward_fields=forward_fields, adjoint_now=adjoint_now, adjoint_prev=adjoint_prev, courant_sq=courant_sq, receiver_cells=receiver_cells, traces=traces)


def laplace(padded):
    center = padded[2:-2, 2:-2, 2:-2]
    total = -7.5 * center
    total = total + (4.0 / 3.0) * (padded[3:-1, 2:-2, 2:-2] + padded[1:-3, 2:-2, 2:-2])
    total = total - (1.0 / 12.0) * (padded[4:, 2:-2, 2:-2] + padded[:-4, 2:-2, 2:-2])
    total = total + (4.0 / 3.0) * (padded[2:-2, 3:-1, 2:-2] + padded[2:-2, 1:-3, 2:-2])
    total = total - (1.0 / 12.0) * (padded[2:-2, 4:, 2:-2] + padded[2:-2, :-4, 2:-2])
    total = total + (4.0 / 3.0) * (padded[2:-2, 2:-2, 3:-1] + padded[2:-2, 2:-2, 1:-3])
    total = total - (1.0 / 12.0) * (padded[2:-2, 2:-2, 4:] + padded[2:-2, 2:-2, :-4])
    return total


def truncate(field, axis, keep):
    length = field.shape[axis]
    index = jnp.arange(length)
    signed = jnp.where(index < length - length // 2, index, index - length)
    if length % 2 == 0:
        signed = jnp.where(index < length // 2, index, index - length)
    mask = (jnp.abs(signed) < keep // 2).astype(field.dtype)
    shape = [1, 1, 1]
    shape[axis] = length
    spectrum = jnp.fft.fft(field, axis=axis) * mask.reshape(shape)
    return jnp.fft.ifft(spectrum, axis=axis).real


def reference(forward_fields, adjoint_now, adjoint_prev, courant_sq, receiver_cells, traces):
    shape = adjoint_now.shape
    bx = jnp.arange(BRICKS_X, dtype=jnp.int32)[:, None, None]
    by = jnp.arange(BRICKS_Y, dtype=jnp.int32)[None, :, None]
    local = receiver_cells
    gx = bx * CX + local // (CY * NZ)
    gy = by * CY + (local // NZ) % CY
    gz = local % NZ
    flat_cells = ((gx * NY + gy) * NZ + gz).reshape(-1).astype(jnp.int32)
    gradient = jnp.zeros(shape, jnp.float32)
    now, prev = adjoint_now, adjoint_prev
    for step in range(STEPS):
        lap = laplace(jnp.pad(now, 2))
        gradient = gradient + forward_fields[step].astype(jnp.float32) * lap
        nxt = 2.0 * now - prev + courant_sq * lap
        nxt = nxt.reshape(-1).at[flat_cells].add(traces[:, :, step, :].reshape(-1)).reshape(shape)
        prev, now = now, nxt
    field = gradient
    field = truncate(field, 0, KX)
    field = truncate(field, 1, KY)
    field = truncate(field, 2, KZ)
    return field.astype(jnp.float32), now, prev
```

```python
import functools

import jax
import jax.numpy as jnp
import numpy as np
from jax import lax
from jax.experimental import pallas as pl
from jax.experimental.pallas import tpu as pltpu
from jax.sharding import PartitionSpec as P

STEPS = 4
KX = 128
KY = 128
KZ = 64
GROUP = 4
ROWS = 256
TWELFTH = 1.0 / 12.0

HBM = pl.BlockSpec(memory_space=pltpu.HBM)
VMEM = pl.BlockSpec(memory_space=pltpu.VMEM)
SMEM = pl.BlockSpec(memory_space=pltpu.SMEM)
DMA = pltpu.SemaphoreType.DMA
NT = (((1,), (1,)), ((), ()))
NN = (((1,), (0,)), ((), ()))
TN = (((0,), (0,)), ((), ()))


def split(value):
    high = value.astype(jnp.bfloat16)
    low = (value - high.astype(jnp.float32)).astype(jnp.bfloat16)
    return high, low


def dot(left, right, dims):
    return lax.dot_general(left, right, dims, preferred_element_type=jnp.float32)


def dot3(left, right, dims):
    return (
        dot(left[0], right[0], dims)
        + dot(left[1], right[0], dims)
        + dot(left[0], right[1], dims)
    )


def basis(count, length):
    half = count // 2
    cells = np.arange(length, dtype=np.int64)[None, :]
    modes = np.arange(count, dtype=np.int64)[:, None]
    freq = np.where(modes < half, modes, modes - half + 1)
    phase = (freq * cells % length) * (2.0 * np.pi / length)
    values = np.sqrt(2.0 / length) * np.where(modes < half, np.cos(phase), np.sin(phase))
    values[0] = np.sqrt(1.0 / length)
    values[count - 1] = 0.0
    return values


def bands(size_y, size_z):
    def far(size):
        one = lax.broadcasted_iota(jnp.int32, (size, size), 0)
        two = lax.broadcasted_iota(jnp.int32, (size, size), 1)
        return jnp.abs(one - two), one // size_y == two // size_y

    gap, _ = far(size_z)
    band_z = jnp.where(gap == 0, -90.0, jnp.where(gap == 1, 16.0, jnp.where(gap == 2, -1.0, 0.0)))
    gap, same = far(ROWS)
    band_y = jnp.where(gap == 1, 16.0, jnp.where(gap == 2, -1.0, 0.0))
    band_y = jnp.where(same, band_y, 0.0)
    return band_z.astype(jnp.bfloat16), band_y.astype(jnp.bfloat16)


def pack(now, x_low, x_high, y_low, y_high, first, last, sems):
    size_x, size_y, _ = now.shape
    copies = [
        pltpu.make_async_copy(now.at[0:2], x_low, sems.at[0]),
        pltpu.make_async_copy(now.at[size_x - 2 : size_x], x_high, sems.at[1]),
        pltpu.make_async_copy(now.at[:, 0:8], first, sems.at[2]),
        pltpu.make_async_copy(now.at[:, size_y - 8 : size_y], last, sems.at[3]),
    ]
    for copy in copies:
        copy.start()
    for copy in copies:
        copy.wait()
    y_low[...] = first[:, 0:2, :]
    y_high[...] = last[:, 6:8, :]


def x_changes(inside, x_low, x_high, size_x):
    before = [jnp.where(inside[0] > 0, x_low[i], 0.0) for i in range(2)]
    after = [jnp.where(inside[1] > 0, x_high[i], 0.0) for i in range(2)]
    return {
        0: 16.0 * before[1] - before[0],
        1: -before[1],
        size_x - 2: -after[0],
        size_x - 1: 16.0 * after[0] - after[1],
    }


def y_tiles(inside, y_low, y_high, x):
    size_z = y_low.shape[2]
    line = lax.broadcasted_iota(jnp.int32, (8, size_z), 0)
    low = jnp.where(inside[2] > 0, y_low[x], 0.0)
    near = jnp.broadcast_to(low[1:2], (8, size_z))
    far = jnp.broadcast_to(low[0:1], (8, size_z))
    first = jnp.where(line == 0, 16.0 * near - far, jnp.where(line == 1, -near, 0.0))
    high = jnp.where(inside[3] > 0, y_high[x], 0.0)
    near = jnp.broadcast_to(high[0:1], (8, size_z))
    far = jnp.broadcast_to(high[1:2], (8, size_z))
    last = jnp.where(line == 7, 16.0 * near - far, jnp.where(line == 6, -near, 0.0))
    return first, last


def with_change(value, x, x_change, tiles):
    size_y = value.shape[0]
    parts = [value[0:8] + tiles[0], value[8 : size_y - 8], value[size_y - 8 : size_y] + tiles[1]]
    value = jnp.concatenate(parts, axis=0)
    return value + x_change[x] if x in x_change else value


def faces_after(inside, x_low, x_high, y_low, y_high, courant, base, lap, out_x_low, out_x_high, out_y_low, out_y_high):
    size_x, size_y, _ = base.shape
    x_change = x_changes(inside, x_low, x_high, size_x)
    for x in range(size_x):
        tiles = y_tiles(inside, y_low, y_high, x)
        if x in x_change:
            value = with_change(lap[x], x, x_change, tiles)
            value = base[x] + (courant[x] * TWELFTH) * value
            out = out_x_low if x < 2 else out_x_high
            out[x % 2] = value
            first, last = value[0:8], value[size_y - 8 : size_y]
        else:
            first = base[x, 0:8] + (courant[x, 0:8] * TWELFTH) * (lap[x, 0:8] + tiles[0])
            end = slice(size_y - 8, size_y)
            last = base[x, end] + (courant[x, end] * TWELFTH) * (lap[x, end] + tiles[1])
        out_y_low[x] = first[0:2]
        out_y_high[x] = last[6:8]


def injection(step, cells, traces, size_z):
    spots = cells[...]
    value = traces[pl.ds(step, 1), :]
    top = value.astype(jnp.bfloat16)
    rest = value - top.astype(jnp.float32)
    mid = rest.astype(jnp.bfloat16)
    low = (rest - mid.astype(jnp.float32)).astype(jnp.bfloat16)
    depth = lax.broadcasted_iota(jnp.int32, (size_z, spots.shape[1]), 0)
    here = depth == spots % size_z
    parts = [
        jnp.where(here, part.astype(jnp.float32), 0.0).astype(jnp.bfloat16)
        for part in (top, mid, low)
    ]
    line = lax.broadcasted_iota(jnp.int32, (ROWS, spots.shape[1]), 0)

    def block(first_row):
        hits = jnp.where(line == spots // size_z - first_row, 1.0, 0.0).astype(jnp.bfloat16)
        return sum(dot(hits, part, NT) for part in parts)

    return block


def laplace_block(now, first, layers, band_z, band_y):
    size_x, size_y, size_z = now.shape
    center = now[first : first + layers].reshape(ROWS, size_z)
    high, low = split(center)
    lap = dot(high, band_z, NN) + dot(low, band_z, NN)
    lap = lap + dot(band_y, high, NN) + dot(band_y, low, NN)
    lap = lap.reshape(layers, size_y, size_z)
    out = []
    for layer in range(layers):
        x = first + layer
        near = [now[x + d] for d in (-1, 1) if 0 <= x + d < size_x]
        far = [now[x + d] for d in (-2, 2) if 0 <= x + d < size_x]
        value = lap[layer] + 16.0 * functools.reduce(jnp.add, near)
        out.append(value - functools.reduce(jnp.add, far))
    return out


def first_step(now_hbm, prev_hbm, courant_hbm, forward_hbm, cells, traces, now, courant, forward, base, lap, prev, sems):
    size_x, size_y, size_z = now.shape
    layers = ROWS // size_y
    blocks = size_x // layers
    copies = []
    for source, target, row in ((now_hbm, now, 0), (prev_hbm, prev, 1)):
        for b in range(blocks):
            part = pl.ds(b * layers, layers)
            copies.append(pltpu.make_async_copy(source.at[part], target.at[part], sems.at[row, b]))
    others = [
        pltpu.make_async_copy(courant_hbm, courant, sems.at[2, 0]),
        pltpu.make_async_copy(forward_hbm.at[0], forward, sems.at[2, 1]),
    ]
    for b in range(blocks):
        copies[b].start()
        copies[blocks + b].start()
    for copy in others:
        copy.start()
    band_z, band_y = bands(size_y, size_z)
    added = injection(0, cells, traces, size_z)
    copies[0].wait()
    for b in range(blocks):
        if b + 1 < blocks:
            copies[b + 1].wait()
        copies[blocks + b].wait()
        inject = added(b * ROWS).reshape(layers, size_y, size_z)
        for i, value in enumerate(laplace_block(now, b * layers, layers, band_z, band_y)):
            x = b * layers + i
            lap[x] = value
            base[x] = (2.0 * now[x] - prev[x]) + inject[i]
    for copy in others:
        copy.wait()


def later_step(step, has_gradient, *refs):
    inside, x_low, x_high, y_low, y_high, base_in, lap_in, prev, courant, forward_in, forward_hbm, cells, traces, *refs = refs
    gradient_in = refs.pop(0) if has_gradient else None
    last = step == STEPS - 1
    if last:
        now, lap, gradient, forward, sem = refs
    else:
        now, lap, gradient, forward, base, sem = refs
    size_x, size_y, size_z = now.shape
    layers = ROWS // size_y
    copy = pltpu.make_async_copy(forward_hbm.at[step], forward, sem)
    copy.start()
    band_z, band_y = bands(size_y, size_z)
    x_change = x_changes(inside, x_low, x_high, size_x)
    for x in range(size_x):
        value = with_change(lap_in[x], x, x_change, y_tiles(inside, y_low, y_high, x))
        now[x] = base_in[x] + (courant[x] * TWELFTH) * value
        value = forward_in[x].astype(jnp.float32) * value
        gradient[x] = gradient_in[x] + value if has_gradient else value
    added = None if last else injection(step, cells, traces, size_z)
    if last:
        copy.wait()
    for b in range(size_x // layers):
        inject = None if last else added(b * ROWS).reshape(layers, size_y, size_z)
        for i, value in enumerate(laplace_block(now, b * layers, layers, band_z, band_y)):
            x = b * layers + i
            lap[x] = value
            if last:
                gradient[x] += forward[x].astype(jnp.float32) * value
            else:
                base[x] = (2.0 * now[x] - prev[x]) + inject[i]
    if not last:
        copy.wait()


def finish(inside, x_low, x_high, y_low, y_high, now, lap, prev, courant, cells, traces, next_hbm, now_hbm, nxt, sems):
    size_x, size_y, size_z = now.shape
    layers = ROWS // size_y
    keep = pltpu.make_async_copy(now, now_hbm, sems.at[0])
    keep.start()
    added = injection(STEPS - 1, cells, traces, size_z)
    x_change = x_changes(inside, x_low, x_high, size_x)
    copies = []
    for b in range(size_x // layers):
        inject = added(b * ROWS).reshape(layers, size_y, size_z)
        for i in range(layers):
            x = b * layers + i
            value = with_change(lap[x], x, x_change, y_tiles(inside, y_low, y_high, x))
            base = (2.0 * now[x] - prev[x]) + inject[i]
            nxt[x] = base + (courant[x] * TWELFTH) * value
        part = pl.ds(b * layers, layers)
        copies.append(pltpu.make_async_copy(nxt.at[part], next_hbm.at[part], sems.at[1 + b]))
        copies[-1].start()
    for copy in copies:
        copy.wait()
    keep.wait()


def project_z(inside, x_low, x_high, y_low, y_high, forward, gradient, table_z, coef):
    size_x, size_y, _ = gradient.shape
    table = split(table_z[...])
    x_change = x_changes(inside, x_low, x_high, size_x)
    for s in range(8):
        lines = []
        for x in range(s, size_x, 8):
            first, last = y_tiles(inside, y_low, y_high, x)
            scale = forward[x].astype(jnp.float32)
            tiles = (scale[0:8] * first, scale[size_y - 8 : size_y] * last)
            value = with_change(gradient[x], x, {}, tiles)
            lines.append(value + scale * x_change[x] if x in x_change else value)
        coef[:, s, :] = dot3(table, split(jnp.concatenate(lines, axis=0)), NT)


def project_y(chunks, table_y, out, plane):
    count = chunks.shape[0] // GROUP
    for r in range(GROUP):
        for q in range(4):
            pieces = [chunks[r * count + c][:, q * 32 : (q + 1) * 32] for c in range(count)]
            plane[pl.ds((r * 4 + q) * 8, 8), :] = jnp.concatenate(pieces, axis=1)
    out[...] = dot3(split(plane[...]), split(table_y[...]), NT)


def smooth_plane(own, one, two, three, table_x, table_y, chunks, plane):
    total = None
    for k, part in enumerate((own, one, two, three)):
        term = dot3(split(table_x[k]), split(part[...]), NN)
        total = term if total is None else total + term
    plane[...] = dot3(split(total), split(table_y[...]), NN)
    count = chunks.shape[0] // GROUP
    for r in range(GROUP):
        for c in range(count):
            pieces = [plane[pl.ds((r * 4 + q) * 8, 8), c * 32 : (c + 1) * 32] for q in range(4)]
            chunks[r * count + c] = jnp.concatenate(pieces, axis=1)


def expand_z(coef, table_z, out, lines, sems):
    _, size_y, size_z = out.shape
    high, low = split(table_z[...])
    table = jnp.concatenate([high, high, low], axis=0)
    copies = []
    for s in range(8):
        high, low = split(coef[:, s, :])
        value = dot(jnp.concatenate([high, low, high], axis=0), table, TN)
        lines[s] = value.reshape(4, size_y, size_z)
        for q in range(4):
            copies.append(pltpu.make_async_copy(lines.at[s, q], out.at[q * 8 + s], sems.at[s, q]))
            copies[-1].start()
    for copy in copies:
        copy.wait()


def call(kernel, out_shape, specs, out_specs=None, scratch=(), room=24, **cost):
    return pl.pallas_call(
        kernel,
        out_shape=out_shape,
        in_specs=specs,
        out_specs=out_specs or jax.tree.map(lambda _: VMEM, out_shape),
        scratch_shapes=scratch,
        compiler_params=pltpu.CompilerParams(vmem_limit_bytes=int(room * 2**20)),
        cost_estimate=pl.CostEstimate(transcendentals=0, **cost),
    )


def per_device(forward_fields, adjoint_now, adjoint_prev, courant_sq, receiver_cells, traces):
    shape = adjoint_now.shape
    size_x, size_y, size_z = shape
    rows, cols = lax.axis_size("row"), lax.axis_size("col")
    row, col = lax.axis_index("row"), lax.axis_index("col")
    inside = jnp.stack([row > 0, row < rows - 1, col > 0, col < cols - 1]).astype(jnp.int32)
    spots = receiver_cells.reshape(1, -1)
    values = traces.reshape(STEPS, -1)
    basis_z = basis(KZ, size_z)
    table_z = jnp.asarray(basis_z, jnp.float32)
    table_z_scaled = jnp.asarray(basis_z * TWELFTH, jnp.float32)
    table_y = jnp.asarray(basis(KY, cols * size_y), jnp.float32)
    basis_x = basis(KX, rows * size_x)
    low_pass = basis_x.T @ basis_x
    own = GROUP * size_x
    parts = rows // GROUP
    table_x = jnp.asarray(
        np.stack([low_pass[:own, k * own : (k + 1) * own] for k in range(parts)]), jnp.float32
    )

    field = jax.ShapeDtypeStruct(shape, jnp.float32)
    half_field = jax.ShapeDtypeStruct(shape, jnp.bfloat16)
    x_face = jax.ShapeDtypeStruct((2, size_y, size_z), jnp.float32)
    y_face = jax.ShapeDtypeStruct((size_x, 2, size_z), jnp.float32)
    chunks = jax.ShapeDtypeStruct((KZ, 8, 128), jnp.float32)
    ring = [[(i, (i + 1) % n) for i in range(n)] for n in (rows, cols)]
    back = [[(b, a) for a, b in pairs] for pairs in ring]
    heavy = dict(flops=2 * 10**9, bytes_accessed=7 * 2**20)
    light = dict(flops=10**6, bytes_accessed=2**18)
    strip = pltpu.VMEM((size_x, 8, size_z), jnp.float32)
    whole = pltpu.VMEM(shape, jnp.float32)
    blocks = size_x * size_y // ROWS

    faces = call(
        pack, (x_face, x_face, y_face, y_face), [HBM], scratch=[strip, strip, DMA((4,))], room=57, **light
    )(adjoint_now)
    halo = gradient = prev = None
    for step in range(STEPS):
        sent = (
            lax.ppermute(faces[1], "row", ring[0]),
            lax.ppermute(faces[0], "row", back[0]),
            lax.ppermute(faces[3], "col", ring[1]),
            lax.ppermute(faces[2], "col", back[1]),
        )
        if step == 0:
            now, courant, forward, base, lap = call(
                first_step,
                (field, field, half_field, field, field),
                [HBM] * 4 + [VMEM] * 2,
                scratch=[whole, DMA((3, blocks))],
                room=49,
                **heavy,
            )(adjoint_now, adjoint_prev, courant_sq, forward_fields, spots, values)
        else:
            last = step == STEPS - 1
            operands = (inside, *halo, base, lap, now, courant, forward, forward_fields, spots, values)
            specs = [SMEM] + [VMEM] * 9 + [HBM] + [VMEM] * 2
            if step > 1:
                operands, specs = operands + (gradient,), specs + [VMEM]
            prev = now
            results = call(
                functools.partial(later_step, step, step > 1),
                (field, field, field, half_field) + (() if last else (field,)),
                specs,
                scratch=[DMA(())],
                **heavy,
            )(*operands)
            now, lap, gradient, forward = results[:4]
            base = None if last else results[4]
        halo = sent
        if step < STEPS - 1:
            faces = call(
                faces_after, (x_face, x_face, y_face, y_face), [SMEM] + [VMEM] * 7, **light
            )(inside, *halo, courant, base, lap)
    coef = call(project_z, chunks, [SMEM] + [VMEM] * 7, **light)(
        inside, *halo, forward, gradient, table_z_scaled
    )
    final_now, final_prev = call(
        finish,
        (field, field),
        [SMEM] + [VMEM] * 10,
        out_specs=(HBM, HBM),
        scratch=[whole, DMA((1 + blocks,))],
        **heavy,
    )(inside, *halo, now, lap, prev, courant, spots, values)

    groups = [
        [(g * GROUP + r) * cols + c for r in range(GROUP) for c in range(cols)] for g in range(parts)
    ]
    both = ("row", "col")
    coef = lax.all_to_all(coef, both, 0, 0, axis_index_groups=groups, tiled=True)
    plane = jax.ShapeDtypeStruct((own, KY), jnp.float32)
    wide = pltpu.VMEM((own, cols * size_y), jnp.float32)
    mine = call(project_y, plane, [VMEM] * 2, scratch=[wide], **light)(coef, table_y)
    others = [
        lax.ppermute(mine, "row", [((i + k * GROUP) % rows, i) for i in range(rows)])
        for k in range(1, parts)
    ]
    coef = call(smooth_plane, chunks, [VMEM] * 6, scratch=[wide], **light)(
        mine, *others, table_x, table_y
    )
    coef = lax.all_to_all(coef, both, 0, 0, axis_index_groups=groups, tiled=True)
    smoothed = call(
        expand_z,
        field,
        [VMEM] * 2,
        out_specs=HBM,
        scratch=[pltpu.VMEM((8, 4, size_y, size_z), jnp.float32), DMA((8, 4))],
        **light,
    )(coef, table_z)
    return (smoothed, final_now, final_prev)


def solution(mesh):
    in_specs = (
        P(None, "row", "col", None),
        P("row", "col", None),
        P("row", "col", None),
        P("row", "col", None),
        P("row", "col", None),
        P("row", "col", None, None),
    )
    out_specs = (P("row", "col", None), P("row", "col", None), P("row", "col", None))
    return jax.shard_map(
        per_device, mesh=mesh, in_specs=in_specs, out_specs=out_specs, check_vma=False
    )
```

```python
import functools

import jax
import jax.numpy as jnp
import numpy as np
from jax import lax
from jax.experimental import pallas as pl
from jax.experimental.pallas import tpu as pltpu
from jax.sharding import PartitionSpec as P

STEPS = 4
KX = 128
KY = 128
KZ = 64
GROUP = 4
ROWS = 256
TWELFTH = 1.0 / 12.0
PACK_ROOM = 52
FIRST_ROOM = 50

HBM = pl.BlockSpec(memory_space=pltpu.HBM)
VMEM = pl.BlockSpec(memory_space=pltpu.VMEM)
SMEM = pl.BlockSpec(memory_space=pltpu.SMEM)
DMA = pltpu.SemaphoreType.DMA
NT = (((1,), (1,)), ((), ()))
NN = (((1,), (0,)), ((), ()))
TN = (((0,), (0,)), ((), ()))


def split(value):
    high = value.astype(jnp.bfloat16)
    low = (value - high.astype(jnp.float32)).astype(jnp.bfloat16)
    return high, low


def dot(left, right, dims):
    return lax.dot_general(left, right, dims, preferred_element_type=jnp.float32)


def dot3(left, right, dims):
    return (
        dot(left[0], right[0], dims)
        + dot(left[1], right[0], dims)
        + dot(left[0], right[1], dims)
    )


def basis(count, length):
    half = count // 2
    cells = np.arange(length, dtype=np.int64)[None, :]
    modes = np.arange(count, dtype=np.int64)[:, None]
    freq = np.where(modes < half, modes, modes - half + 1)
    phase = (freq * cells % length) * (2.0 * np.pi / length)
    values = np.sqrt(2.0 / length) * np.where(modes < half, np.cos(phase), np.sin(phase))
    values[0] = np.sqrt(1.0 / length)
    values[count - 1] = 0.0
    return values


def bands(size_y, size_z):
    def far(size):
        one = lax.broadcasted_iota(jnp.int32, (size, size), 0)
        two = lax.broadcasted_iota(jnp.int32, (size, size), 1)
        return jnp.abs(one - two), one // size_y == two // size_y

    gap, _ = far(size_z)
    band_z = jnp.where(gap == 0, -90.0, jnp.where(gap == 1, 16.0, jnp.where(gap == 2, -1.0, 0.0)))
    gap, same = far(ROWS)
    band_y = jnp.where(gap == 1, 16.0, jnp.where(gap == 2, -1.0, 0.0))
    band_y = jnp.where(same, band_y, 0.0)
    return band_z.astype(jnp.bfloat16), band_y.astype(jnp.bfloat16)


def with_flags(rows, cols, kernel, spot, *refs):
    row, col = spot[0] >> (cols.bit_length() - 1), spot[0] & (cols - 1)
    turn = row & (GROUP - 1)
    flags = [row, rows - 1 - row, col, cols - 1 - col, row & 1, col & 1]
    flags += [turn - (turn ^ k) + GROUP - 1 for k in range(GROUP)]
    kernel(flags, *refs)


def pack(flags, now_hbm, now, x_even, x_odd, y_even, y_odd, sems):
    size_x, size_y, _ = now.shape
    step = size_x // 4
    copies = []
    for b in range(4):
        part = pl.ds(b * step, step)
        copies.append(pltpu.make_async_copy(now_hbm.at[part], now.at[part], sems.at[b]))
        copies[-1].start()
    for b in range(4):
        copies[b].wait()
        part = pl.ds(b * step, step)
        low, high = now[part, 0:2, :], now[part, size_y - 2 : size_y, :]
        y_even[part] = jnp.where(flags[5] > 0, low, high)
        y_odd[part] = jnp.where(flags[5] > 0, high, low)
    low, high = now[0:2], now[size_x - 2 : size_x]
    x_even[...] = jnp.where(flags[4] > 0, low, high)
    x_odd[...] = jnp.where(flags[4] > 0, high, low)


def x_changes(flags, x_even, x_odd, size_x):
    odd = flags[4] > 0
    before = [jnp.where(odd, x_even[i], x_odd[i]) for i in range(2)]
    after = [jnp.where(odd, x_odd[i], x_even[i]) for i in range(2)]
    before = [jnp.where(flags[0] > 0, value, 0.0) for value in before]
    after = [jnp.where(flags[1] > 0, value, 0.0) for value in after]
    return {
        0: 16.0 * before[1] - before[0],
        1: -before[1],
        size_x - 2: -after[0],
        size_x - 1: 16.0 * after[0] - after[1],
    }


def y_tiles(flags, y_even, y_odd, x):
    size_z = y_even.shape[2]
    line = lax.broadcasted_iota(jnp.int32, (8, size_z), 0)
    odd = flags[5] > 0
    low = jnp.where(flags[2] > 0, jnp.where(odd, y_even[x], y_odd[x]), 0.0)
    near = jnp.broadcast_to(low[1:2], (8, size_z))
    far = jnp.broadcast_to(low[0:1], (8, size_z))
    first = jnp.where(line == 0, 16.0 * near - far, jnp.where(line == 1, -near, 0.0))
    high = jnp.where(flags[3] > 0, jnp.where(odd, y_odd[x], y_even[x]), 0.0)
    near = jnp.broadcast_to(high[0:1], (8, size_z))
    far = jnp.broadcast_to(high[1:2], (8, size_z))
    last = jnp.where(line == 7, 16.0 * near - far, jnp.where(line == 6, -near, 0.0))
    return first, last


def with_change(value, x, x_change, tiles):
    size_y = value.shape[0]
    parts = [value[0:8] + tiles[0], value[8 : size_y - 8], value[size_y - 8 : size_y] + tiles[1]]
    value = jnp.concatenate(parts, axis=0)
    return value + x_change[x] if x in x_change else value


def faces_after(flags, x_even, x_odd, y_even, y_odd, courant, base, lap, out_x_even, out_x_odd, out_y_even, out_y_odd):
    size_x, size_y, _ = base.shape
    x_change = x_changes(flags, x_even, x_odd, size_x)
    layers = {}
    for x in range(size_x):
        tiles = y_tiles(flags, y_even, y_odd, x)
        if x in x_change:
            value = with_change(lap[x], x, x_change, tiles)
            layers[x] = value = base[x] + (courant[x] * TWELFTH) * value
            first, last = value[0:8], value[size_y - 8 : size_y]
        else:
            first = base[x, 0:8] + (courant[x, 0:8] * TWELFTH) * (lap[x, 0:8] + tiles[0])
            end = slice(size_y - 8, size_y)
            last = base[x, end] + (courant[x, end] * TWELFTH) * (lap[x, end] + tiles[1])
        low, high = first[0:2], last[6:8]
        out_y_even[x] = jnp.where(flags[5] > 0, low, high)
        out_y_odd[x] = jnp.where(flags[5] > 0, high, low)
    for i in range(2):
        low, high = layers[i], layers[size_x - 2 + i]
        out_x_even[i] = jnp.where(flags[4] > 0, low, high)
        out_x_odd[i] = jnp.where(flags[4] > 0, high, low)


def injection(step, cells, traces, size_z):
    spots = cells[...]
    value = traces[pl.ds(step, 1), :]
    top = value.astype(jnp.bfloat16)
    rest = value - top.astype(jnp.float32)
    mid = rest.astype(jnp.bfloat16)
    depth = lax.broadcasted_iota(jnp.int32, (size_z, spots.shape[1]), 0)
    here = depth == spots % size_z
    parts = [
        jnp.where(here, part.astype(jnp.float32), 0.0).astype(jnp.bfloat16)
        for part in (top, mid)
    ]
    line = lax.broadcasted_iota(jnp.int32, (ROWS, spots.shape[1]), 0)

    def block(first_row):
        hits = jnp.where(line == spots // size_z - first_row, 1.0, 0.0).astype(jnp.bfloat16)
        return sum(dot(hits, part, NT) for part in parts)

    return block


def laplace_block(now, first, layers, band_z, band_y):
    size_x, size_y, size_z = now.shape
    center = now[first : first + layers].reshape(ROWS, size_z)
    high, low = split(center)
    lap = dot(high, band_z, NN) + dot(low, band_z, NN)
    lap = lap + dot(band_y, high, NN) + dot(band_y, low, NN)
    lap = lap.reshape(layers, size_y, size_z)
    out = []
    for layer in range(layers):
        x = first + layer
        near = [now[x + d] for d in (-1, 1) if 0 <= x + d < size_x]
        far = [now[x + d] for d in (-2, 2) if 0 <= x + d < size_x]
        value = lap[layer] + 16.0 * functools.reduce(jnp.add, near)
        out.append(value - functools.reduce(jnp.add, far))
    return out


def first_step(now, prev_hbm, cells, traces, base, lap, prev, sems):
    size_x, size_y, size_z = now.shape
    layers = ROWS // size_y
    blocks = size_x // layers
    copies = []
    for b in range(blocks):
        part = pl.ds(b * layers, layers)
        copies.append(pltpu.make_async_copy(prev_hbm.at[part], prev.at[part], sems.at[b]))
        copies[-1].start()
    band_z, band_y = bands(size_y, size_z)
    added = injection(0, cells, traces, size_z)
    for b in range(blocks):
        inject = added(b * ROWS).reshape(layers, size_y, size_z)
        for i, value in enumerate(laplace_block(now, b * layers, layers, band_z, band_y)):
            x = b * layers + i
            lap[x] = value
            base[x] = 2.0 * now[x] + inject[i]
    for b in range(blocks):
        copies[b].wait()
        part = slice(b * layers, (b + 1) * layers)
        base[part] = base[part] - prev[part]


def later_step(step, flags, *refs):
    x_even, x_odd, y_even, y_odd, base_in, lap_in, prev, courant, forward, cells, traces, *refs = refs
    gradient_in = refs.pop(0) if step > 1 else None
    last = step == STEPS - 1
    now, lap, gradient = refs[:3]
    base = None if last else refs[3]
    size_x, size_y, size_z = now.shape
    layers = ROWS // size_y
    band_z, band_y = bands(size_y, size_z)
    x_change = x_changes(flags, x_even, x_odd, size_x)
    for x in range(size_x):
        value = with_change(lap_in[x], x, x_change, y_tiles(flags, y_even, y_odd, x))
        now[x] = base_in[x] + (courant[x] * TWELFTH) * value
        value = forward[step - 1, x].astype(jnp.float32) * value
        gradient[x] = gradient_in[x] + value if step > 1 else value
    added = None if last else injection(step, cells, traces, size_z)
    for b in range(size_x // layers):
        inject = None if last else added(b * ROWS).reshape(layers, size_y, size_z)
        for i, value in enumerate(laplace_block(now, b * layers, layers, band_z, band_y)):
            x = b * layers + i
            lap[x] = value
            if last:
                gradient[x] += forward[step, x].astype(jnp.float32) * value
            else:
                base[x] = (2.0 * now[x] - prev[x]) + inject[i]


def finish(flags, x_even, x_odd, y_even, y_odd, now, lap, prev, courant, cells, traces, next_hbm, now_hbm, nxt, sems):
    size_x, size_y, size_z = now.shape
    layers = ROWS // size_y
    keep = pltpu.make_async_copy(now, now_hbm, sems.at[0])
    keep.start()
    added = injection(STEPS - 1, cells, traces, size_z)
    x_change = x_changes(flags, x_even, x_odd, size_x)
    copies = []
    for b in range(size_x // layers):
        inject = added(b * ROWS).reshape(layers, size_y, size_z)
        for i in range(layers):
            x = b * layers + i
            value = with_change(lap[x], x, x_change, y_tiles(flags, y_even, y_odd, x))
            base = (2.0 * now[x] - prev[x]) + inject[i]
            nxt[x] = base + (courant[x] * TWELFTH) * value
        part = pl.ds(b * layers, layers)
        copies.append(pltpu.make_async_copy(nxt.at[part], next_hbm.at[part], sems.at[1 + b]))
        copies[-1].start()
    for copy in copies:
        copy.wait()
    keep.wait()


def project_z(flags, x_even, x_odd, y_even, y_odd, forward, gradient, table_z, coef):
    size_x, size_y, _ = gradient.shape
    table = split(table_z[...])
    x_change = x_changes(flags, x_even, x_odd, size_x)
    for s in range(8):
        lines = []
        for x in range(s, size_x, 8):
            first, last = y_tiles(flags, y_even, y_odd, x)
            scale = forward[STEPS - 1, x].astype(jnp.float32)
            tiles = (scale[0:8] * first, scale[size_y - 8 : size_y] * last)
            value = with_change(gradient[x], x, {}, tiles)
            lines.append(value + scale * x_change[x] if x in x_change else value)
        coef[:, s, :] = dot3(table, split(jnp.concatenate(lines, axis=0)), NT)


def project_y(chunks, table_y, out, plane):
    count = chunks.shape[0] // GROUP
    for r in range(GROUP):
        for q in range(4):
            pieces = [chunks[r * count + c][:, q * 32 : (q + 1) * 32] for c in range(count)]
            plane[pl.ds((r * 4 + q) * 8, 8), :] = jnp.concatenate(pieces, axis=1)
    out[...] = dot3(split(plane[...]), split(table_y[...]), NT)


def smooth_plane(flags, own, one, two, three, table_x, table_y, chunks_hbm, plane, chunks, sems):
    high, low = split(jnp.concatenate([own[...], one[...], two[...], three[...]], axis=0))
    tables = [split(table_x[flags[6 + k]]) for k in range(GROUP)]
    left_high = jnp.concatenate([table[0] for table in tables], axis=1)
    left_low = jnp.concatenate([table[1] for table in tables], axis=1)
    total = dot3((left_high, left_low), (high, low), NN)
    plane[...] = dot3(split(total), split(table_y[...]), NN)
    count = chunks.shape[0] // GROUP
    copies = []
    for r in range(GROUP):
        for c in range(count):
            pieces = [plane[pl.ds((r * 4 + q) * 8, 8), c * 32 : (c + 1) * 32] for q in range(4)]
            chunks[r * count + c] = jnp.concatenate(pieces, axis=1)
        part = pl.ds(r * count, count)
        copies.append(pltpu.make_async_copy(chunks.at[part], chunks_hbm.at[part], sems.at[r]))
        copies[-1].start()
    for copy in copies:
        copy.wait()


def expand_z(coef, table_z, out, lines, sems):
    _, size_y, size_z = out.shape
    high, low = split(table_z[...])
    table = jnp.concatenate([high, high, low], axis=0)
    copies = []
    for s in range(8):
        high, low = split(coef[:, s, :])
        value = dot(jnp.concatenate([high, low, high], axis=0), table, TN)
        lines[s] = value.reshape(4, size_y, size_z)
        for q in range(4):
            copies.append(pltpu.make_async_copy(lines.at[s, q], out.at[q * 8 + s], sems.at[s, q]))
            copies[-1].start()
    for copy in copies:
        copy.wait()


def call(kernel, out_shape, specs, out_specs=None, scratch=(), room=24, **cost):
    return pl.pallas_call(
        kernel,
        out_shape=out_shape,
        in_specs=specs,
        out_specs=out_specs or jax.tree.map(lambda _: VMEM, out_shape),
        scratch_shapes=scratch,
        compiler_params=pltpu.CompilerParams(vmem_limit_bytes=int(room * 2**20)),
        cost_estimate=pl.CostEstimate(transcendentals=0, **cost),
    )


def per_device(forward_fields, adjoint_now, adjoint_prev, courant_sq, receiver_cells, traces):
    shape = adjoint_now.shape
    size_x, size_y, size_z = shape
    rows, cols = lax.axis_size("row"), lax.axis_size("col")
    both = ("row", "col")
    spot = lax.axis_index(both).reshape(1)
    placed = functools.partial(functools.partial, with_flags, rows, cols)
    spots = receiver_cells.reshape(1, -1)
    values = traces.reshape(STEPS, -1)
    basis_z = basis(KZ, size_z)
    table_z = jnp.asarray(basis_z, jnp.float32)
    table_z_scaled = jnp.asarray(basis_z * TWELFTH, jnp.float32)
    table_y = jnp.asarray(basis(KY, cols * size_y), jnp.float32)
    basis_x = basis(KX, rows * size_x)
    low_pass = (basis_x.T @ basis_x)[0]
    span = rows // GROUP
    own = span * size_x
    place = (np.arange(span)[:, None] * GROUP * size_x + np.arange(size_x)[None, :]).reshape(-1)
    gap = place[:, None] - place[None, :]
    table_x = jnp.asarray(
        np.stack([low_pass[(gap + k * size_x) % low_pass.size] for k in range(1 - GROUP, GROUP)]),
        jnp.float32,
    )

    field = jax.ShapeDtypeStruct(shape, jnp.float32)
    x_face = jax.ShapeDtypeStruct((2, size_y, size_z), jnp.float32)
    y_face = jax.ShapeDtypeStruct((size_x, 2, size_z), jnp.float32)
    chunks = jax.ShapeDtypeStruct((KZ, 8, 128), jnp.float32)
    swaps = [[], [], [], []]
    for r in range(rows):
        for c in range(cols):
            up, right = r + 2 * (r % 2) - 1, c + 2 * (c % 2) - 1
            targets = (
                (r ^ 1, c),
                (up, c) if 0 <= up < rows else (r, c ^ 1),
                (r, c ^ 1),
                (r, right) if 0 <= right < cols else (r ^ 1, c),
            )
            for pairs, (to_row, to_col) in zip(swaps, targets):
                pairs.append((r * cols + c, to_row * cols + to_col))
    heavy = dict(flops=2 * 10**9, bytes_accessed=7 * 2**20)
    light = dict(flops=10**6, bytes_accessed=2**18)
    whole = pltpu.VMEM(shape, jnp.float32)
    blocks = size_x * size_y // ROWS

    now, *faces = call(
        placed(pack),
        (field, x_face, x_face, y_face, y_face),
        [SMEM, HBM],
        scratch=[DMA((4,))],
        room=PACK_ROOM,
        **light,
    )(spot, adjoint_now)
    halo = gradient = prev = None
    for step in range(STEPS):
        sent = [lax.ppermute(face, both, pairs) for face, pairs in zip(faces, swaps)]
        if step == 0:
            base, lap = call(
                first_step,
                (field, field),
                [VMEM, HBM, VMEM, VMEM],
                scratch=[whole, DMA((blocks,))],
                room=FIRST_ROOM,
                **heavy,
            )(now, adjoint_prev, spots, values)
        else:
            last = step == STEPS - 1
            operands = (spot, *halo, base, lap, now, courant_sq, forward_fields, spots, values)
            if step > 1:
                operands += (gradient,)
            prev = now
            results = call(
                placed(functools.partial(later_step, step)),
                (field,) * (3 if last else 4),
                [SMEM] + [VMEM] * (len(operands) - 1),
                **heavy,
            )(*operands)
            now, lap, gradient = results[:3]
            base = None if last else results[3]
        halo = sent
        if step < STEPS - 1:
            faces = call(
                placed(faces_after), (x_face, x_face, y_face, y_face), [SMEM] + [VMEM] * 7, **light
            )(spot, *halo, courant_sq, base, lap)
    coef = call(placed(project_z), chunks, [SMEM] + [VMEM] * 7, **light)(
        spot, *halo, forward_fields, gradient, table_z_scaled
    )
    final_now, final_prev = call(
        placed(finish),
        (field, field),
        [SMEM] + [VMEM] * 10,
        out_specs=(HBM, HBM),
        scratch=[whole, DMA((1 + blocks,))],
        **heavy,
    )(spot, *halo, now, lap, prev, courant_sq, spots, values)

    groups = [
        [(m * GROUP + g) * cols + c for m in range(span) for c in range(cols)] for g in range(GROUP)
    ]
    coef = lax.all_to_all(coef, both, 0, 0, axis_index_groups=groups, tiled=True)
    plane = jax.ShapeDtypeStruct((own, KY), jnp.float32)
    wide = pltpu.VMEM((own, cols * size_y), jnp.float32)
    mine = call(project_y, plane, [VMEM] * 2, scratch=[wide], **light)(coef, table_y)
    others = [
        lax.ppermute(mine, "row", [(i, i ^ k) for i in range(rows)]) for k in range(1, GROUP)
    ]
    coef = call(
        placed(smooth_plane),
        chunks,
        [SMEM] + [VMEM] * 6,
        out_specs=HBM,
        scratch=[wide, pltpu.VMEM(chunks.shape, jnp.float32), DMA((GROUP,))],
        **light,
    )(
        spot, mine, *others, table_x, table_y
    )
    coef = lax.all_to_all(coef, both, 0, 0, axis_index_groups=groups, tiled=True)
    smoothed = call(
        expand_z,
        field,
        [VMEM] * 2,
        out_specs=HBM,
        scratch=[pltpu.VMEM((8, 4, size_y, size_z), jnp.float32), DMA((8, 4))],
        **light,
    )(coef, table_z)
    return (smoothed, final_now, final_prev)


def solution(mesh):
    in_specs = (
        P(None, "row", "col", None),
        P("row", "col", None),
        P("row", "col", None),
        P("row", "col", None),
        P("row", "col", None),
        P("row", "col", None, None),
    )
    out_specs = (P("row", "col", None), P("row", "col", None), P("row", "col", None))
    return jax.shard_map(
        per_device, mesh=mesh, in_specs=in_specs, out_specs=out_specs, check_vma=False
    )
```

```python
import functools

import jax
import jax.numpy as jnp
import numpy as np
from jax import lax
from jax.experimental import pallas as pl
from jax.experimental.pallas import tpu as pltpu
from jax.sharding import PartitionSpec as P

STEPS = 4
KX = 128
KY = 128
KZ = 64
GROUP = 4
ROWS = 256
TWELFTH = 1.0 / 12.0
PACK_ROOM = 52
FIRST_ROOM = 50
ORDER = (1, 3, 2, 0)

HBM = pl.BlockSpec(memory_space=pltpu.HBM)
VMEM = pl.BlockSpec(memory_space=pltpu.VMEM)
SMEM = pl.BlockSpec(memory_space=pltpu.SMEM)
DMA = pltpu.SemaphoreType.DMA
NT = (((1,), (1,)), ((), ()))
NN = (((1,), (0,)), ((), ()))
TN = (((0,), (0,)), ((), ()))


def split(value):
    high = value.astype(jnp.bfloat16)
    low = (value - high.astype(jnp.float32)).astype(jnp.bfloat16)
    return high, low


def dot(left, right, dims):
    return lax.dot_general(left, right, dims, preferred_element_type=jnp.float32)


def dot3(left, right, dims):
    return (
        dot(left[0], right[0], dims)
        + dot(left[1], right[0], dims)
        + dot(left[0], right[1], dims)
    )


def basis(count, length):
    half = count // 2
    cells = np.arange(length, dtype=np.int64)[None, :]
    modes = np.arange(count, dtype=np.int64)[:, None]
    freq = np.where(modes < half, modes, modes - half + 1)
    phase = (freq * cells % length) * (2.0 * np.pi / length)
    values = np.sqrt(2.0 / length) * np.where(modes < half, np.cos(phase), np.sin(phase))
    values[0] = np.sqrt(1.0 / length)
    values[count - 1] = 0.0
    return values


def bands(size_y, size_z):
    def far(size):
        one = lax.broadcasted_iota(jnp.int32, (size, size), 0)
        two = lax.broadcasted_iota(jnp.int32, (size, size), 1)
        return jnp.abs(one - two), one // size_y == two // size_y

    gap, _ = far(size_z)
    band_z = jnp.where(gap == 0, -90.0, jnp.where(gap == 1, 16.0, jnp.where(gap == 2, -1.0, 0.0)))
    gap, same = far(ROWS)
    band_y = jnp.where(gap == 1, 16.0, jnp.where(gap == 2, -1.0, 0.0))
    band_y = jnp.where(same, band_y, 0.0)
    return band_z.astype(jnp.bfloat16), band_y.astype(jnp.bfloat16)


def with_flags(rows, cols, kernel, spot, *refs):
    row, col = spot[0] >> (cols.bit_length() - 1), spot[0] & (cols - 1)
    turn = row & (GROUP - 1)
    flags = [row, rows - 1 - row, col, cols - 1 - col, row & 1, col & 1]
    flags += [turn - (turn ^ k) + GROUP - 1 for k in range(GROUP)]
    kernel(flags, *refs)


def pack(flags, now_hbm, now, x_odd, y_odd, y_even, x_even, sems):
    size_x, size_y, _ = now.shape
    step = size_x // 4
    copies = []
    for b in range(4):
        part = pl.ds(b * step, step)
        copies.append(pltpu.make_async_copy(now_hbm.at[part], now.at[part], sems.at[b]))
        copies[-1].start()
    for b in range(4):
        copies[b].wait()
        part = pl.ds(b * step, step)
        low, high = now[part, 0:2, :], now[part, size_y - 2 : size_y, :]
        y_even[part] = jnp.where(flags[5] > 0, low, high)
        y_odd[part] = jnp.where(flags[5] > 0, high, low)
    low, high = now[0:2], now[size_x - 2 : size_x]
    x_even[...] = jnp.where(flags[4] > 0, low, high)
    x_odd[...] = jnp.where(flags[4] > 0, high, low)


def x_changes(flags, x_even, x_odd, size_x):
    odd = flags[4] > 0
    before = [jnp.where(odd, x_even[i], x_odd[i]) for i in range(2)]
    after = [jnp.where(odd, x_odd[i], x_even[i]) for i in range(2)]
    before = [jnp.where(flags[0] > 0, value, 0.0) for value in before]
    after = [jnp.where(flags[1] > 0, value, 0.0) for value in after]
    return {
        0: 16.0 * before[1] - before[0],
        1: -before[1],
        size_x - 2: -after[0],
        size_x - 1: 16.0 * after[0] - after[1],
    }


def y_tiles(flags, y_even, y_odd, x):
    size_z = y_even.shape[2]
    line = lax.broadcasted_iota(jnp.int32, (8, size_z), 0)
    odd = flags[5] > 0
    low = jnp.where(flags[2] > 0, jnp.where(odd, y_even[x], y_odd[x]), 0.0)
    near = jnp.broadcast_to(low[1:2], (8, size_z))
    far = jnp.broadcast_to(low[0:1], (8, size_z))
    first = jnp.where(line == 0, 16.0 * near - far, jnp.where(line == 1, -near, 0.0))
    high = jnp.where(flags[3] > 0, jnp.where(odd, y_odd[x], y_even[x]), 0.0)
    near = jnp.broadcast_to(high[0:1], (8, size_z))
    far = jnp.broadcast_to(high[1:2], (8, size_z))
    last = jnp.where(line == 7, 16.0 * near - far, jnp.where(line == 6, -near, 0.0))
    return first, last


def with_change(value, x, x_change, tiles):
    size_y = value.shape[0]
    parts = [value[0:8] + tiles[0], value[8 : size_y - 8], value[size_y - 8 : size_y] + tiles[1]]
    value = jnp.concatenate(parts, axis=0)
    return value + x_change[x] if x in x_change else value


def faces_after(flags, x_odd, y_odd, y_even, x_even, courant, base, lap, out_x_odd, out_y_odd, out_y_even, out_x_even):
    size_x, size_y, _ = base.shape
    x_change = x_changes(flags, x_even, x_odd, size_x)
    layers = {}
    for x in range(size_x):
        tiles = y_tiles(flags, y_even, y_odd, x)
        if x in x_change:
            value = with_change(lap[x], x, x_change, tiles)
            layers[x] = value = base[x] + (courant[x] * TWELFTH) * value
            first, last = value[0:8], value[size_y - 8 : size_y]
        else:
            first = base[x, 0:8] + (courant[x, 0:8] * TWELFTH) * (lap[x, 0:8] + tiles[0])
            end = slice(size_y - 8, size_y)
            last = base[x, end] + (courant[x, end] * TWELFTH) * (lap[x, end] + tiles[1])
        low, high = first[0:2], last[6:8]
        out_y_even[x] = jnp.where(flags[5] > 0, low, high)
        out_y_odd[x] = jnp.where(flags[5] > 0, high, low)
    for i in range(2):
        low, high = layers[i], layers[size_x - 2 + i]
        out_x_even[i] = jnp.where(flags[4] > 0, low, high)
        out_x_odd[i] = jnp.where(flags[4] > 0, high, low)


def injection(step, cells, traces, size_z):
    spots = cells[0]
    value = traces[0, 0, pl.ds(step, 1), :]
    top = value.astype(jnp.bfloat16)
    rest = value - top.astype(jnp.float32)
    mid = rest.astype(jnp.bfloat16)
    depth = lax.broadcasted_iota(jnp.int32, (size_z, spots.shape[1]), 0)
    here = depth == spots % size_z
    parts = [
        jnp.where(here, part.astype(jnp.float32), 0.0).astype(jnp.bfloat16)
        for part in (top, mid)
    ]
    line = lax.broadcasted_iota(jnp.int32, (ROWS, spots.shape[1]), 0)

    def block(first_row):
        hits = jnp.where(line == spots // size_z - first_row, 1.0, 0.0).astype(jnp.bfloat16)
        return sum(dot(hits, part, NT) for part in parts)

    return block


def laplace_block(now, first, layers, band_z, band_y):
    size_x, size_y, size_z = now.shape
    center = now[first : first + layers].reshape(ROWS, size_z)
    high, low = split(center)
    lap = dot(high, band_z, NN) + dot(low, band_z, NN)
    lap = lap + dot(band_y, high, NN) + dot(band_y, low, NN)
    lap = lap.reshape(layers, size_y, size_z)
    out = []
    for layer in range(layers):
        x = first + layer
        near = [now[x + d] for d in (-1, 1) if 0 <= x + d < size_x]
        far = [now[x + d] for d in (-2, 2) if 0 <= x + d < size_x]
        value = lap[layer] + 16.0 * functools.reduce(jnp.add, near)
        out.append(value - functools.reduce(jnp.add, far))
    return out


def first_step(now, prev_hbm, cells, traces, base, lap, prev, sems):
    size_x, size_y, size_z = now.shape
    layers = ROWS // size_y
    blocks = size_x // layers
    copies = []
    for b in range(blocks):
        part = pl.ds(b * layers, layers)
        copies.append(pltpu.make_async_copy(prev_hbm.at[part], prev.at[part], sems.at[b]))
        copies[-1].start()
    band_z, band_y = bands(size_y, size_z)
    added = injection(0, cells, traces, size_z)
    for b in range(blocks):
        inject = added(b * ROWS).reshape(layers, size_y, size_z)
        for i, value in enumerate(laplace_block(now, b * layers, layers, band_z, band_y)):
            x = b * layers + i
            lap[x] = value
            base[x] = 2.0 * now[x] + inject[i]
    for b in range(blocks):
        copies[b].wait()
        part = slice(b * layers, (b + 1) * layers)
        base[part] = base[part] - prev[part]


def later_step(step, flags, *refs):
    x_odd, y_odd, y_even, x_even, base_in, lap_in, prev, courant, forward, cells, traces, *refs = refs
    gradient_in = refs.pop(0) if step > 1 else None
    last = step == STEPS - 1
    now, lap, gradient = refs[:3]
    base = None if last else refs[3]
    size_x, size_y, size_z = now.shape
    layers = ROWS // size_y
    band_z, band_y = bands(size_y, size_z)
    x_change = x_changes(flags, x_even, x_odd, size_x)
    for x in range(size_x):
        value = with_change(lap_in[x], x, x_change, y_tiles(flags, y_even, y_odd, x))
        now[x] = base_in[x] + (courant[x] * TWELFTH) * value
        value = forward[step - 1, x].astype(jnp.float32) * value
        gradient[x] = gradient_in[x] + value if step > 1 else value
    added = None if last else injection(step, cells, traces, size_z)
    for b in range(size_x // layers):
        inject = None if last else added(b * ROWS).reshape(layers, size_y, size_z)
        for i, value in enumerate(laplace_block(now, b * layers, layers, band_z, band_y)):
            x = b * layers + i
            lap[x] = value
            if last:
                gradient[x] += forward[step, x].astype(jnp.float32) * value
            else:
                base[x] = (2.0 * now[x] - prev[x]) + inject[i]


def finish(flags, x_odd, y_odd, y_even, x_even, now, lap, prev, courant, cells, traces, next_hbm, now_hbm, nxt, sems):
    size_x, size_y, size_z = now.shape
    layers = ROWS // size_y
    keep = pltpu.make_async_copy(now, now_hbm, sems.at[0])
    keep.start()
    added = injection(STEPS - 1, cells, traces, size_z)
    x_change = x_changes(flags, x_even, x_odd, size_x)
    copies = []
    for b in range(size_x // layers):
        inject = added(b * ROWS).reshape(layers, size_y, size_z)
        for i in range(layers):
            x = b * layers + i
            value = with_change(lap[x], x, x_change, y_tiles(flags, y_even, y_odd, x))
            base = (2.0 * now[x] - prev[x]) + inject[i]
            nxt[x] = base + (courant[x] * TWELFTH) * value
        part = pl.ds(b * layers, layers)
        copies.append(pltpu.make_async_copy(nxt.at[part], next_hbm.at[part], sems.at[1 + b]))
        copies[-1].start()
    for copy in copies:
        copy.wait()
    keep.wait()


def project_z(flags, x_odd, y_odd, y_even, x_even, forward, gradient, table_z, coef):
    size_x, size_y, _ = gradient.shape
    table = split(table_z[...])
    x_change = x_changes(flags, x_even, x_odd, size_x)
    for s in range(8):
        lines = []
        for x in range(4 * s, 4 * s + 4):
            first, last = y_tiles(flags, y_even, y_odd, x)
            scale = forward[STEPS - 1, x].astype(jnp.float32)
            tiles = (scale[0:8] * first, scale[size_y - 8 : size_y] * last)
            value = with_change(gradient[x], x, {}, tiles)
            lines.append(value + scale * x_change[x] if x in x_change else value)
        coef[:, s, :] = dot3(table, split(jnp.concatenate(lines, axis=0)), NT)


def project_y(chunks, table_y, out, plane):
    count = chunks.shape[0] // GROUP
    for r in range(GROUP):
        for q in range(4):
            pieces = [chunks[r * count + c][:, q * 32 : (q + 1) * 32] for c in range(count)]
            plane[pl.ds((r * 4 + q) * 8, 8), :] = jnp.concatenate(pieces, axis=1)
    out[...] = dot3(split(plane[...]), split(table_y[...]), NT)


def smooth_plane(flags, own, one, two, three, table_x, table_y, chunks_hbm, plane, chunks, sems):
    high, low = split(jnp.concatenate([own[...], one[...], two[...], three[...]], axis=0))
    tables = [split(table_x[flags[6 + k]]) for k in range(GROUP)]
    left_high = jnp.concatenate([table[0] for table in tables], axis=1)
    left_low = jnp.concatenate([table[1] for table in tables], axis=1)
    total = dot3((left_high, left_low), (high, low), NN)
    plane[...] = dot3(split(total), split(table_y[...]), NN)
    count = chunks.shape[0] // GROUP
    copies = []
    for r in range(GROUP):
        for c in range(count):
            pieces = [plane[pl.ds((r * 4 + q) * 8, 8), c * 32 : (c + 1) * 32] for q in range(4)]
            chunks[r * count + c] = jnp.concatenate(pieces, axis=1)
        part = pl.ds(r * count, count)
        copies.append(pltpu.make_async_copy(chunks.at[part], chunks_hbm.at[part], sems.at[r]))
        copies[-1].start()
    for copy in copies:
        copy.wait()


def expand_z(coef, table_z, out, lines, sems):
    _, size_y, size_z = out.shape
    high, low = split(table_z[...])
    table = jnp.concatenate([high, high, low], axis=0)
    copies = []
    for s in range(8):
        high, low = split(coef[:, s, :])
        value = dot(jnp.concatenate([high, low, high], axis=0), table, TN)
        lines[s] = value.reshape(4, size_y, size_z)
        copies.append(pltpu.make_async_copy(lines.at[s], out.at[pl.ds(4 * s, 4)], sems.at[s]))
        copies[-1].start()
    for copy in copies:
        copy.wait()


def call(kernel, out_shape, specs, out_specs=None, scratch=(), room=24, **cost):
    return pl.pallas_call(
        kernel,
        out_shape=out_shape,
        in_specs=specs,
        out_specs=out_specs or jax.tree.map(lambda _: VMEM, out_shape),
        scratch_shapes=scratch,
        compiler_params=pltpu.CompilerParams(vmem_limit_bytes=int(room * 2**20)),
        cost_estimate=pl.CostEstimate(transcendentals=0, **cost),
    )


def per_device(forward_fields, adjoint_now, adjoint_prev, courant_sq, receiver_cells, traces):
    shape = adjoint_now.shape
    size_x, size_y, size_z = shape
    rows, cols = lax.axis_size("row"), lax.axis_size("col")
    both = ("row", "col")
    spot = lax.axis_index(both).reshape(1)
    placed = functools.partial(functools.partial, with_flags, rows, cols)
    basis_z = basis(KZ, size_z)
    table_z = jnp.asarray(basis_z, jnp.float32)
    table_z_scaled = jnp.asarray(basis_z * TWELFTH, jnp.float32)
    table_y = jnp.asarray(basis(KY, cols * size_y), jnp.float32)
    basis_x = basis(KX, rows * size_x)
    low_pass = (basis_x.T @ basis_x)[0]
    span = rows // GROUP
    own = span * size_x
    cells = (np.arange(4)[:, None] + 4 * np.arange(8)[None, :]).reshape(-1)
    place = (np.arange(span)[:, None] * GROUP * size_x + cells[None, :]).reshape(-1)
    gap = place[:, None] - place[None, :]
    table_x = jnp.asarray(
        np.stack([low_pass[(gap + k * size_x) % low_pass.size] for k in range(1 - GROUP, GROUP)]),
        jnp.float32,
    )

    field = jax.ShapeDtypeStruct(shape, jnp.float32)
    x_face = jax.ShapeDtypeStruct((2, size_y, size_z), jnp.float32)
    y_face = jax.ShapeDtypeStruct((size_x, 2, size_z), jnp.float32)
    chunks = jax.ShapeDtypeStruct((KZ, 8, 128), jnp.float32)
    swaps = [[], [], [], []]
    for r in range(rows):
        for c in range(cols):
            up, right = r + 2 * (r % 2) - 1, c + 2 * (c % 2) - 1
            targets = (
                (r ^ 1, c),
                (up, c) if 0 <= up < rows else (r, c ^ 1),
                (r, c ^ 1),
                (r, right) if 0 <= right < cols else (r ^ 1, c),
            )
            for pairs, (to_row, to_col) in zip(swaps, targets):
                pairs.append((r * cols + c, to_row * cols + to_col))
    heavy = dict(flops=2 * 10**9, bytes_accessed=7 * 2**20)
    light = dict(flops=10**6, bytes_accessed=2**18)
    whole = pltpu.VMEM(shape, jnp.float32)
    blocks = size_x * size_y // ROWS

    now, *faces = call(
        placed(pack),
        (field, x_face, y_face, y_face, x_face),
        [SMEM, HBM],
        scratch=[DMA((4,))],
        room=PACK_ROOM,
        **light,
    )(spot, adjoint_now)
    spots, values = receiver_cells, traces
    halo = gradient = prev = None
    for step in range(STEPS):
        sent = [lax.ppermute(face, both, swaps[i]) for i, face in zip(ORDER, faces)]
        if step == 0:
            base, lap = call(
                first_step,
                (field, field),
                [VMEM, HBM, VMEM, VMEM],
                scratch=[whole, DMA((blocks,))],
                room=FIRST_ROOM,
                **heavy,
            )(now, adjoint_prev, spots, values)
        else:
            last = step == STEPS - 1
            operands = (spot, *halo, base, lap, now, courant_sq, forward_fields, spots, values)
            if step > 1:
                operands += (gradient,)
            prev = now
            results = call(
                placed(functools.partial(later_step, step)),
                (field,) * (3 if last else 4),
                [SMEM] + [VMEM] * (len(operands) - 1),
                **heavy,
            )(*operands)
            now, lap, gradient = results[:3]
            base = None if last else results[3]
        halo = sent
        if step < STEPS - 1:
            faces = call(
                placed(faces_after), (x_face, y_face, y_face, x_face), [SMEM] + [VMEM] * 7, **light
            )(spot, *halo, courant_sq, base, lap)
    coef = call(placed(project_z), chunks, [SMEM] + [VMEM] * 7, **light)(
        spot, *halo, forward_fields, gradient, table_z_scaled
    )
    final_now, final_prev = call(
        placed(finish),
        (field, field),
        [SMEM] + [VMEM] * 10,
        out_specs=(HBM, HBM),
        scratch=[whole, DMA((1 + blocks,))],
        **heavy,
    )(spot, *halo, now, lap, prev, courant_sq, spots, values)

    groups = [
        [(m * GROUP + g) * cols + c for m in range(span) for c in range(cols)] for g in range(GROUP)
    ]
    coef = lax.all_to_all(coef, both, 0, 0, axis_index_groups=groups, tiled=True)
    plane = jax.ShapeDtypeStruct((own, KY), jnp.float32)
    wide = pltpu.VMEM((own, cols * size_y), jnp.float32)
    mine = call(project_y, plane, [VMEM] * 2, scratch=[wide], **light)(coef, table_y)
    beside, across = ([(i, i ^ k) for i in range(rows)] for k in (1, 2))
    two = lax.ppermute(mine, "row", across)
    one = lax.ppermute(mine, "row", beside)
    others = (one, two, lax.ppermute(two, "row", beside))
    coef = call(
        placed(smooth_plane),
        chunks,
        [SMEM] + [VMEM] * 6,
        out_specs=HBM,
        scratch=[wide, pltpu.VMEM(chunks.shape, jnp.float32), DMA((GROUP,))],
        **light,
    )(
        spot, mine, *others, table_x, table_y
    )
    coef = lax.all_to_all(coef, both, 0, 0, axis_index_groups=groups, tiled=True)
    smoothed = call(
        expand_z,
        field,
        [VMEM] * 2,
        out_specs=HBM,
        scratch=[pltpu.VMEM((8, 4, size_y, size_z), jnp.float32), DMA((8,))],
        **light,
    )(coef, table_z)
    return (smoothed, final_now, final_prev)


def solution(mesh):
    in_specs = (
        P(None, "row", "col", None),
        P("row", "col", None),
        P("row", "col", None),
        P("row", "col", None),
        P("row", "col", None),
        P("row", "col", None, None),
    )
    out_specs = (P("row", "col", None), P("row", "col", None), P("row", "col", None))
    return jax.shard_map(
        per_device, mesh=mesh, in_specs=in_specs, out_specs=out_specs, check_vma=False
    )
```

```python
import functools

import jax
import jax.numpy as jnp
import numpy as np
from jax import lax
from jax.experimental import pallas as pl
from jax.experimental.pallas import tpu as pltpu
from jax.sharding import PartitionSpec as P

STEPS = 4
KX = 128
KY = 128
KZ = 64
GROUP = 4
ROWS = 256
TWELFTH = 1.0 / 12.0
PACK_ROOM = 52
FIRST_ROOM = 50
ORDER = (1, 3, 2, 0)

HBM = pl.BlockSpec(memory_space=pltpu.HBM)
VMEM = pl.BlockSpec(memory_space=pltpu.VMEM)
SMEM = pl.BlockSpec(memory_space=pltpu.SMEM)
DMA = pltpu.SemaphoreType.DMA
NT = (((1,), (1,)), ((), ()))
NN = (((1,), (0,)), ((), ()))
TN = (((0,), (0,)), ((), ()))


def split(value):
    high = value.astype(jnp.bfloat16)
    low = (value - high.astype(jnp.float32)).astype(jnp.bfloat16)
    return high, low


def dot(left, right, dims):
    return lax.dot_general(left, right, dims, preferred_element_type=jnp.float32)


def dot3(left, right, dims):
    return (
        dot(left[0], right[0], dims)
        + dot(left[1], right[0], dims)
        + dot(left[0], right[1], dims)
    )


def basis(count, length):
    half = count // 2
    cells = np.arange(length, dtype=np.int64)[None, :]
    modes = np.arange(count, dtype=np.int64)[:, None]
    freq = np.where(modes < half, modes, modes - half + 1)
    phase = (freq * cells % length) * (2.0 * np.pi / length)
    values = np.sqrt(2.0 / length) * np.where(modes < half, np.cos(phase), np.sin(phase))
    values[0] = np.sqrt(1.0 / length)
    values[count - 1] = 0.0
    return values


def bands(size_y, size_z):
    def far(size):
        one = lax.broadcasted_iota(jnp.int32, (size, size), 0)
        two = lax.broadcasted_iota(jnp.int32, (size, size), 1)
        return jnp.abs(one - two), one // size_y == two // size_y

    gap, _ = far(size_z)
    band_z = jnp.where(gap == 0, -90.0, jnp.where(gap == 1, 16.0, jnp.where(gap == 2, -1.0, 0.0)))
    gap, same = far(ROWS)
    band_y = jnp.where(gap == 1, 16.0, jnp.where(gap == 2, -1.0, 0.0))
    band_y = jnp.where(same, band_y, 0.0)
    return band_z.astype(jnp.bfloat16), band_y.astype(jnp.bfloat16)


def with_flags(rows, cols, kernel, spot, *refs):
    row, col = spot[0] >> (cols.bit_length() - 1), spot[0] & (cols - 1)
    turn = row & (GROUP - 1)
    flags = [row, rows - 1 - row, col, cols - 1 - col, row & 1, col & 1]
    flags += [turn - (turn ^ k) + GROUP - 1 for k in range(GROUP)]
    kernel(flags, *refs)


def pack(flags, now_hbm, now, x_odd, y_odd, y_even, x_even, sems):
    size_x, size_y, _ = now.shape
    step = size_x // 4
    copies = []
    for b in range(4):
        part = pl.ds(b * step, step)
        copies.append(pltpu.make_async_copy(now_hbm.at[part], now.at[part], sems.at[b]))
        copies[-1].start()
    for b in range(4):
        copies[b].wait()
        part = pl.ds(b * step, step)
        low, high = now[part, 0:2, :], now[part, size_y - 2 : size_y, :]
        y_even[part] = jnp.where(flags[5] > 0, low, high)
        y_odd[part] = jnp.where(flags[5] > 0, high, low)
    low, high = now[0:2], now[size_x - 2 : size_x]
    x_even[...] = jnp.where(flags[4] > 0, low, high)
    x_odd[...] = jnp.where(flags[4] > 0, high, low)


def x_changes(flags, x_even, x_odd, size_x):
    odd = flags[4] > 0
    before = [jnp.where(odd, x_even[i], x_odd[i]) for i in range(2)]
    after = [jnp.where(odd, x_odd[i], x_even[i]) for i in range(2)]
    before = [jnp.where(flags[0] > 0, value, 0.0) for value in before]
    after = [jnp.where(flags[1] > 0, value, 0.0) for value in after]
    return {
        0: 16.0 * before[1] - before[0],
        1: -before[1],
        size_x - 2: -after[0],
        size_x - 1: 16.0 * after[0] - after[1],
    }


def y_tiles(flags, y_even, y_odd, x):
    size_z = y_even.shape[2]
    line = lax.broadcasted_iota(jnp.int32, (8, size_z), 0)
    odd = flags[5] > 0
    low = jnp.where(flags[2] > 0, jnp.where(odd, y_even[x], y_odd[x]), 0.0)
    near = jnp.broadcast_to(low[1:2], (8, size_z))
    far = jnp.broadcast_to(low[0:1], (8, size_z))
    first = jnp.where(line == 0, 16.0 * near - far, jnp.where(line == 1, -near, 0.0))
    high = jnp.where(flags[3] > 0, jnp.where(odd, y_odd[x], y_even[x]), 0.0)
    near = jnp.broadcast_to(high[0:1], (8, size_z))
    far = jnp.broadcast_to(high[1:2], (8, size_z))
    last = jnp.where(line == 7, 16.0 * near - far, jnp.where(line == 6, -near, 0.0))
    return first, last


def with_change(value, x, x_change, tiles):
    size_y = value.shape[0]
    parts = [value[0:8] + tiles[0], value[8 : size_y - 8], value[size_y - 8 : size_y] + tiles[1]]
    value = jnp.concatenate(parts, axis=0)
    return value + x_change[x] if x in x_change else value


def faces_after(flags, x_odd, y_odd, y_even, x_even, courant, base, lap, out_x_odd, out_y_odd, out_y_even, out_x_even):
    size_x, size_y, _ = base.shape
    x_change = x_changes(flags, x_even, x_odd, size_x)
    layers = {}
    for x in range(size_x):
        tiles = y_tiles(flags, y_even, y_odd, x)
        if x in x_change:
            value = with_change(lap[x], x, x_change, tiles)
            layers[x] = value = base[x] + (courant[x] * TWELFTH) * value
            first, last = value[0:8], value[size_y - 8 : size_y]
        else:
            first = base[x, 0:8] + (courant[x, 0:8] * TWELFTH) * (lap[x, 0:8] + tiles[0])
            end = slice(size_y - 8, size_y)
            last = base[x, end] + (courant[x, end] * TWELFTH) * (lap[x, end] + tiles[1])
        low, high = first[0:2], last[6:8]
        out_y_even[x] = jnp.where(flags[5] > 0, low, high)
        out_y_odd[x] = jnp.where(flags[5] > 0, high, low)
    for i in range(2):
        low, high = layers[i], layers[size_x - 2 + i]
        out_x_even[i] = jnp.where(flags[4] > 0, low, high)
        out_x_odd[i] = jnp.where(flags[4] > 0, high, low)


def injection(step, cells, traces, size_z):
    spots = cells[0]
    value = traces[0, 0, pl.ds(step, 1), :]
    top = value.astype(jnp.bfloat16)
    rest = value - top.astype(jnp.float32)
    mid = rest.astype(jnp.bfloat16)
    depth = lax.broadcasted_iota(jnp.int32, (size_z, spots.shape[1]), 0)
    here = depth == spots % size_z
    parts = [
        jnp.where(here, part.astype(jnp.float32), 0.0).astype(jnp.bfloat16)
        for part in (top, mid)
    ]
    line = lax.broadcasted_iota(jnp.int32, (ROWS, spots.shape[1]), 0)

    def block(first_row):
        hits = jnp.where(line == spots // size_z - first_row, 1.0, 0.0).astype(jnp.bfloat16)
        return sum(dot(hits, part, NT) for part in parts)

    return block


def laplace_block(now, first, layers, band_z, band_y):
    size_x, size_y, size_z = now.shape
    center = now[first : first + layers].reshape(ROWS, size_z)
    high, low = split(center)
    lap = dot(high, band_z, NN) + dot(low, band_z, NN)
    lap = lap + dot(band_y, high, NN) + dot(band_y, low, NN)
    lap = lap.reshape(layers, size_y, size_z)
    out = []
    for layer in range(layers):
        x = first + layer
        near = [now[x + d] for d in (-1, 1) if 0 <= x + d < size_x]
        far = [now[x + d] for d in (-2, 2) if 0 <= x + d < size_x]
        value = lap[layer] + 16.0 * functools.reduce(jnp.add, near)
        out.append(value - functools.reduce(jnp.add, far))
    return out


def first_step(now, prev_hbm, cells, traces, base, lap, prev, sems):
    size_x, size_y, size_z = now.shape
    layers = ROWS // size_y
    blocks = size_x // layers
    copies = []
    for b in range(blocks):
        part = pl.ds(b * layers, layers)
        copies.append(pltpu.make_async_copy(prev_hbm.at[part], prev.at[part], sems.at[b]))
        copies[-1].start()
    band_z, band_y = bands(size_y, size_z)
    added = injection(0, cells, traces, size_z)
    for b in range(blocks):
        inject = added(b * ROWS).reshape(layers, size_y, size_z)
        for i, value in enumerate(laplace_block(now, b * layers, layers, band_z, band_y)):
            x = b * layers + i
            lap[x] = value
            base[x] = 2.0 * now[x] + inject[i]
    for b in range(blocks):
        copies[b].wait()
        part = slice(b * layers, (b + 1) * layers)
        base[part] = base[part] - prev[part]


def later_step(step, flags, *refs):
    x_odd, y_odd, y_even, x_even, base_in, lap_in, prev, courant, forward, cells, traces, *refs = refs
    gradient_in = refs.pop(0) if step > 1 else None
    last = step == STEPS - 1
    now, lap, gradient = refs[:3]
    base = None if last else refs[3]
    size_x, size_y, size_z = now.shape
    layers = ROWS // size_y
    band_z, band_y = bands(size_y, size_z)
    x_change = x_changes(flags, x_even, x_odd, size_x)
    for x in range(size_x):
        value = with_change(lap_in[x], x, x_change, y_tiles(flags, y_even, y_odd, x))
        now[x] = base_in[x] + (courant[x] * TWELFTH) * value
        value = forward[step - 1, x].astype(jnp.float32) * value
        gradient[x] = gradient_in[x] + value if step > 1 else value
    added = None if last else injection(step, cells, traces, size_z)
    for b in range(size_x // layers):
        inject = None if last else added(b * ROWS).reshape(layers, size_y, size_z)
        for i, value in enumerate(laplace_block(now, b * layers, layers, band_z, band_y)):
            x = b * layers + i
            lap[x] = value
            if last:
                gradient[x] += forward[step, x].astype(jnp.float32) * value
            else:
                base[x] = (2.0 * now[x] - prev[x]) + inject[i]


def finish(flags, x_odd, y_odd, y_even, x_even, now, lap, prev, courant, cells, traces, next_hbm, now_hbm, nxt, sems):
    size_x, size_y, size_z = now.shape
    layers = ROWS // size_y
    keep = pltpu.make_async_copy(now, now_hbm, sems.at[0])
    keep.start()
    added = injection(STEPS - 1, cells, traces, size_z)
    x_change = x_changes(flags, x_even, x_odd, size_x)
    copies = []
    for b in range(size_x // layers):
        inject = added(b * ROWS).reshape(layers, size_y, size_z)
        for i in range(layers):
            x = b * layers + i
            value = with_change(lap[x], x, x_change, y_tiles(flags, y_even, y_odd, x))
            base = (2.0 * now[x] - prev[x]) + inject[i]
            nxt[x] = base + (courant[x] * TWELFTH) * value
        part = pl.ds(b * layers, layers)
        copies.append(pltpu.make_async_copy(nxt.at[part], next_hbm.at[part], sems.at[1 + b]))
        copies[-1].start()
    for copy in copies:
        copy.wait()
    keep.wait()


def project_z(flags, x_odd, y_odd, y_even, x_even, forward, gradient, table_z, coef):
    size_x, size_y, _ = gradient.shape
    table = split(table_z[...])
    x_change = x_changes(flags, x_even, x_odd, size_x)
    for s in range(8):
        lines = []
        for x in range(4 * s, 4 * s + 4):
            first, last = y_tiles(flags, y_even, y_odd, x)
            scale = forward[STEPS - 1, x].astype(jnp.float32)
            tiles = (scale[0:8] * first, scale[size_y - 8 : size_y] * last)
            value = with_change(gradient[x], x, {}, tiles)
            lines.append(value + scale * x_change[x] if x in x_change else value)
        value = dot3(table, split(jnp.concatenate(lines, axis=0)), NT)
        coef[pl.ds(s, value.shape[0], stride=8), :] = value


def project_y(chunks, table_y, out, plane):
    count = chunks.shape[0] // GROUP
    for r in range(GROUP):
        for q in range(4):
            pieces = [chunks[r * count + c][:, q * 32 : (q + 1) * 32] for c in range(count)]
            plane[pl.ds((r * 4 + q) * 8, 8), :] = jnp.concatenate(pieces, axis=1)
    out[...] = dot3(split(plane[...]), split(table_y[...]), NT)


def smooth_plane(flags, own, one, two, three, table_x, table_y, chunks, plane):
    high, low = split(jnp.concatenate([own[...], one[...], two[...], three[...]], axis=0))
    tables = [split(table_x[flags[6 + k]]) for k in range(GROUP)]
    left_high = jnp.concatenate([table[0] for table in tables], axis=1)
    left_low = jnp.concatenate([table[1] for table in tables], axis=1)
    total = dot3((left_high, left_low), (high, low), NN)
    plane[...] = dot3(split(total), split(table_y[...]), NN)
    count = chunks.shape[0] // GROUP
    for r in range(GROUP):
        for c in range(count):
            pieces = [plane[pl.ds((r * 4 + q) * 8, 8), c * 32 : (c + 1) * 32] for q in range(4)]
            chunks[r * count + c] = jnp.concatenate(pieces, axis=1)


def expand_z(coef, table_z, out, lines, sems):
    _, size_y, size_z = out.shape
    high, low = split(table_z[...])
    table = jnp.concatenate([high, high, low], axis=0)
    copies = []
    for s in range(8):
        high, low = split(coef[pl.ds(s, coef.shape[0] // 8, stride=8), :])
        value = dot(jnp.concatenate([high, low, high], axis=0), table, TN)
        lines[s] = value.reshape(4, size_y, size_z)
        copies.append(pltpu.make_async_copy(lines.at[s], out.at[pl.ds(4 * s, 4)], sems.at[s]))
        copies[-1].start()
    for copy in copies:
        copy.wait()


def call(kernel, out_shape, specs, out_specs=None, scratch=(), room=24, **cost):
    return pl.pallas_call(
        kernel,
        out_shape=out_shape,
        in_specs=specs,
        out_specs=out_specs or jax.tree.map(lambda _: VMEM, out_shape),
        scratch_shapes=scratch,
        compiler_params=pltpu.CompilerParams(vmem_limit_bytes=int(room * 2**20)),
        cost_estimate=pl.CostEstimate(transcendentals=0, **cost),
    )


def per_device(forward_fields, adjoint_now, adjoint_prev, courant_sq, receiver_cells, traces):
    shape = adjoint_now.shape
    size_x, size_y, size_z = shape
    rows, cols = lax.axis_size("row"), lax.axis_size("col")
    both = ("row", "col")
    spot = lax.axis_index(both).reshape(1)
    placed = functools.partial(functools.partial, with_flags, rows, cols)
    basis_z = basis(KZ, size_z)
    table_z = jnp.asarray(basis_z, jnp.float32)
    table_z_scaled = jnp.asarray(basis_z * TWELFTH, jnp.float32)
    table_y = jnp.asarray(basis(KY, cols * size_y), jnp.float32)
    basis_x = basis(KX, rows * size_x)
    low_pass = (basis_x.T @ basis_x)[0]
    span = rows // GROUP
    own = span * size_x
    cells = (np.arange(4)[:, None] + 4 * np.arange(8)[None, :]).reshape(-1)
    place = (np.arange(span)[:, None] * GROUP * size_x + cells[None, :]).reshape(-1)
    gap = place[:, None] - place[None, :]
    table_x = jnp.asarray(
        np.stack([low_pass[(gap + k * size_x) % low_pass.size] for k in range(1 - GROUP, GROUP)]),
        jnp.float32,
    )

    field = jax.ShapeDtypeStruct(shape, jnp.float32)
    x_face = jax.ShapeDtypeStruct((2, size_y, size_z), jnp.float32)
    y_face = jax.ShapeDtypeStruct((size_x, 2, size_z), jnp.float32)
    chunks = jax.ShapeDtypeStruct((KZ, 8, 128), jnp.float32)
    lines = jax.ShapeDtypeStruct((KZ * 8, 128), jnp.float32)
    swaps = [[], [], [], []]
    for r in range(rows):
        for c in range(cols):
            up, right = r + 2 * (r % 2) - 1, c + 2 * (c % 2) - 1
            targets = (
                (r ^ 1, c),
                (up, c) if 0 <= up < rows else (r, c ^ 1),
                (r, c ^ 1),
                (r, right) if 0 <= right < cols else (r ^ 1, c),
            )
            for pairs, (to_row, to_col) in zip(swaps, targets):
                pairs.append((r * cols + c, to_row * cols + to_col))
    heavy = dict(flops=2 * 10**9, bytes_accessed=7 * 2**20)
    light = dict(flops=10**6, bytes_accessed=2**18)
    whole = pltpu.VMEM(shape, jnp.float32)
    blocks = size_x * size_y // ROWS

    now, *faces = call(
        placed(pack),
        (field, x_face, y_face, y_face, x_face),
        [SMEM, HBM],
        scratch=[DMA((4,))],
        room=PACK_ROOM,
        **light,
    )(spot, adjoint_now)
    spots, values = receiver_cells, traces
    halo = gradient = prev = None
    for step in range(STEPS):
        sent = [lax.ppermute(face, both, swaps[i]) for i, face in zip(ORDER, faces)]
        if step == 0:
            base, lap = call(
                first_step,
                (field, field),
                [VMEM, HBM, VMEM, VMEM],
                scratch=[whole, DMA((blocks,))],
                room=FIRST_ROOM,
                **heavy,
            )(now, adjoint_prev, spots, values)
        else:
            last = step == STEPS - 1
            operands = (spot, *halo, base, lap, now, courant_sq, forward_fields, spots, values)
            if step > 1:
                operands += (gradient,)
            prev = now
            results = call(
                placed(functools.partial(later_step, step)),
                (field,) * (3 if last else 4),
                [SMEM] + [VMEM] * (len(operands) - 1),
                **heavy,
            )(*operands)
            now, lap, gradient = results[:3]
            base = None if last else results[3]
        halo = sent
        if step < STEPS - 1:
            faces = call(
                placed(faces_after), (x_face, y_face, y_face, x_face), [SMEM] + [VMEM] * 7, **light
            )(spot, *halo, courant_sq, base, lap)
    coef = call(placed(project_z), lines, [SMEM] + [VMEM] * 7, **light)(
        spot, *halo, forward_fields, gradient, table_z_scaled
    )
    final_now, final_prev = call(
        placed(finish),
        (field, field),
        [SMEM] + [VMEM] * 10,
        out_specs=(HBM, HBM),
        scratch=[whole, DMA((1 + blocks,))],
        **heavy,
    )(spot, *halo, now, lap, prev, courant_sq, spots, values)

    groups = [
        [(m * GROUP + g) * cols + c for m in range(span) for c in range(cols)] for g in range(GROUP)
    ]
    coef = coef.reshape(chunks.shape)
    coef = lax.all_to_all(coef, both, 0, 0, axis_index_groups=groups, tiled=True)
    plane = jax.ShapeDtypeStruct((own, KY), jnp.float32)
    wide = pltpu.VMEM((own, cols * size_y), jnp.float32)
    mine = call(project_y, plane, [VMEM] * 2, scratch=[wide], **light)(coef, table_y)
    beside, across = ([(i, i ^ k) for i in range(rows)] for k in (1, 2))
    two = lax.ppermute(mine, "row", across)
    one = lax.ppermute(mine, "row", beside)
    two, final_now, final_prev = lax.optimization_barrier((two, final_now, final_prev))
    others = (one, two, lax.ppermute(two, "row", beside))
    coef = call(
        placed(smooth_plane),
        chunks,
        [SMEM] + [VMEM] * 6,
        scratch=[wide],
        **light,
    )(
        spot, mine, *others, table_x, table_y
    )
    coef = lax.all_to_all(coef, both, 0, 0, axis_index_groups=groups, tiled=True)
    smoothed = call(
        expand_z,
        field,
        [VMEM] * 2,
        out_specs=HBM,
        scratch=[pltpu.VMEM((8, 4, size_y, size_z), jnp.float32), DMA((8,))],
        **light,
    )(coef.reshape(lines.shape), table_z)
    return (smoothed, final_now, final_prev)


def solution(mesh):
    in_specs = (
        P(None, "row", "col", None),
        P("row", "col", None),
        P("row", "col", None),
        P("row", "col", None),
        P("row", "col", None),
        P("row", "col", None, None),
    )
    out_specs = (P("row", "col", None), P("row", "col", None), P("row", "col", None))
    return jax.shard_map(
        per_device, mesh=mesh, in_specs=in_specs, out_specs=out_specs, check_vma=False
    )
```

```python
import functools

import jax
import jax.numpy as jnp
import numpy as np
from jax import lax
from jax.experimental import pallas as pl
from jax.experimental.pallas import tpu as pltpu
from jax.sharding import PartitionSpec as P

STEPS = 4
KX = 128
KY = 128
KZ = 64
GROUP = 4
ROWS = 256
TWELFTH = 1.0 / 12.0
PACK_ROOM = 52
FIRST_ROOM = 50
ORDER = (3, 1, 2, 0)

HBM = pl.BlockSpec(memory_space=pltpu.HBM)
VMEM = pl.BlockSpec(memory_space=pltpu.VMEM)
SMEM = pl.BlockSpec(memory_space=pltpu.SMEM)
DMA = pltpu.SemaphoreType.DMA
NT = (((1,), (1,)), ((), ()))
NN = (((1,), (0,)), ((), ()))
TN = (((0,), (0,)), ((), ()))


def split(value):
    high = value.astype(jnp.bfloat16)
    low = (value - high.astype(jnp.float32)).astype(jnp.bfloat16)
    return high, low


def dot(left, right, dims):
    return lax.dot_general(left, right, dims, preferred_element_type=jnp.float32)


def dot3(left, right, dims):
    return (
        dot(left[0], right[0], dims)
        + dot(left[1], right[0], dims)
        + dot(left[0], right[1], dims)
    )


def basis(count, length):
    half = count // 2
    cells = np.arange(length, dtype=np.int64)[None, :]
    modes = np.arange(count, dtype=np.int64)[:, None]
    freq = np.where(modes < half, modes, modes - half + 1)
    phase = (freq * cells % length) * (2.0 * np.pi / length)
    values = np.sqrt(2.0 / length) * np.where(modes < half, np.cos(phase), np.sin(phase))
    values[0] = np.sqrt(1.0 / length)
    values[count - 1] = 0.0
    return values


def bands(size_y, size_z):
    def far(size):
        one = lax.broadcasted_iota(jnp.int32, (size, size), 0)
        two = lax.broadcasted_iota(jnp.int32, (size, size), 1)
        return jnp.abs(one - two), one // size_y == two // size_y

    gap, _ = far(size_z)
    band_z = jnp.where(gap == 0, -90.0, jnp.where(gap == 1, 16.0, jnp.where(gap == 2, -1.0, 0.0)))
    gap, same = far(ROWS)
    band_y = jnp.where(gap == 1, 16.0, jnp.where(gap == 2, -1.0, 0.0))
    band_y = jnp.where(same, band_y, 0.0)
    return band_z.astype(jnp.bfloat16), band_y.astype(jnp.bfloat16)


def with_flags(rows, cols, kernel, spot, *refs):
    row, col = spot[0] >> (cols.bit_length() - 1), spot[0] & (cols - 1)
    turn = row & (GROUP - 1)
    flags = [row, rows - 1 - row, col, cols - 1 - col, row & 1, col & 1]
    flags += [turn - (turn ^ k) + GROUP - 1 for k in range(GROUP)]
    kernel(flags, *refs)


def pack(flags, now_hbm, now, y_odd, x_odd, y_even, x_even, sems):
    size_x, size_y, _ = now.shape
    step = size_x // 4
    copies = []
    for b in range(4):
        part = pl.ds(b * step, step)
        copies.append(pltpu.make_async_copy(now_hbm.at[part], now.at[part], sems.at[b]))
        copies[-1].start()
    for b in range(4):
        copies[b].wait()
        part = pl.ds(b * step, step)
        low, high = now[part, 0:2, :], now[part, size_y - 2 : size_y, :]
        y_even[part] = jnp.where(flags[5] > 0, low, high)
        y_odd[part] = jnp.where(flags[5] > 0, high, low)
    low, high = now[0:2], now[size_x - 2 : size_x]
    x_even[...] = jnp.where(flags[4] > 0, low, high)
    x_odd[...] = jnp.where(flags[4] > 0, high, low)


def x_changes(flags, x_even, x_odd, size_x):
    odd = flags[4] > 0
    before = [jnp.where(odd, x_even[i], x_odd[i]) for i in range(2)]
    after = [jnp.where(odd, x_odd[i], x_even[i]) for i in range(2)]
    before = [jnp.where(flags[0] > 0, value, 0.0) for value in before]
    after = [jnp.where(flags[1] > 0, value, 0.0) for value in after]
    return {
        0: 16.0 * before[1] - before[0],
        1: -before[1],
        size_x - 2: -after[0],
        size_x - 1: 16.0 * after[0] - after[1],
    }


def y_tiles(flags, y_even, y_odd, x):
    size_z = y_even.shape[2]
    line = lax.broadcasted_iota(jnp.int32, (8, size_z), 0)
    odd = flags[5] > 0
    low = jnp.where(flags[2] > 0, jnp.where(odd, y_even[x], y_odd[x]), 0.0)
    near = jnp.broadcast_to(low[1:2], (8, size_z))
    far = jnp.broadcast_to(low[0:1], (8, size_z))
    first = jnp.where(line == 0, 16.0 * near - far, jnp.where(line == 1, -near, 0.0))
    high = jnp.where(flags[3] > 0, jnp.where(odd, y_odd[x], y_even[x]), 0.0)
    near = jnp.broadcast_to(high[0:1], (8, size_z))
    far = jnp.broadcast_to(high[1:2], (8, size_z))
    last = jnp.where(line == 7, 16.0 * near - far, jnp.where(line == 6, -near, 0.0))
    return first, last


def with_change(value, x, x_change, tiles):
    size_y = value.shape[0]
    parts = [value[0:8] + tiles[0], value[8 : size_y - 8], value[size_y - 8 : size_y] + tiles[1]]
    value = jnp.concatenate(parts, axis=0)
    return value + x_change[x] if x in x_change else value


def faces_after(flags, y_odd, x_odd, y_even, x_even, courant, base, lap, out_y_odd, out_x_odd, out_y_even, out_x_even):
    size_x, size_y, _ = base.shape
    x_change = x_changes(flags, x_even, x_odd, size_x)
    layers = {}
    for x in range(size_x):
        tiles = y_tiles(flags, y_even, y_odd, x)
        if x in x_change:
            value = with_change(lap[x], x, x_change, tiles)
            layers[x] = value = base[x] + (courant[x] * TWELFTH) * value
            first, last = value[0:8], value[size_y - 8 : size_y]
        else:
            first = base[x, 0:8] + (courant[x, 0:8] * TWELFTH) * (lap[x, 0:8] + tiles[0])
            end = slice(size_y - 8, size_y)
            last = base[x, end] + (courant[x, end] * TWELFTH) * (lap[x, end] + tiles[1])
        low, high = first[0:2], last[6:8]
        out_y_even[x] = jnp.where(flags[5] > 0, low, high)
        out_y_odd[x] = jnp.where(flags[5] > 0, high, low)
    for i in range(2):
        low, high = layers[i], layers[size_x - 2 + i]
        out_x_even[i] = jnp.where(flags[4] > 0, low, high)
        out_x_odd[i] = jnp.where(flags[4] > 0, high, low)


def injection(step, cells, traces, size_z):
    spots = cells[0]
    value = traces[0, 0, pl.ds(step, 1), :]
    top = value.astype(jnp.bfloat16)
    rest = value - top.astype(jnp.float32)
    mid = rest.astype(jnp.bfloat16)
    depth = lax.broadcasted_iota(jnp.int32, (size_z, spots.shape[1]), 0)
    here = depth == spots % size_z
    parts = [
        jnp.where(here, part.astype(jnp.float32), 0.0).astype(jnp.bfloat16)
        for part in (top, mid)
    ]
    line = lax.broadcasted_iota(jnp.int32, (ROWS, spots.shape[1]), 0)

    def block(first_row):
        hits = jnp.where(line == spots // size_z - first_row, 1.0, 0.0).astype(jnp.bfloat16)
        return sum(dot(hits, part, NT) for part in parts)

    return block


def laplace_block(now, first, layers, band_z, band_y):
    size_x, size_y, size_z = now.shape
    center = now[first : first + layers].reshape(ROWS, size_z)
    high, low = split(center)
    lap = dot(high, band_z, NN) + dot(low, band_z, NN)
    lap = lap + dot(band_y, high, NN) + dot(band_y, low, NN)
    lap = lap.reshape(layers, size_y, size_z)
    out = []
    for layer in range(layers):
        x = first + layer
        near = [now[x + d] for d in (-1, 1) if 0 <= x + d < size_x]
        far = [now[x + d] for d in (-2, 2) if 0 <= x + d < size_x]
        value = lap[layer] + 16.0 * functools.reduce(jnp.add, near)
        out.append(value - functools.reduce(jnp.add, far))
    return out


def first_step(now, prev_hbm, cells, traces, base, lap, prev, sems):
    size_x, size_y, size_z = now.shape
    layers = ROWS // size_y
    blocks = size_x // layers
    copies = []
    for b in range(blocks):
        part = pl.ds(b * layers, layers)
        copies.append(pltpu.make_async_copy(prev_hbm.at[part], prev.at[part], sems.at[b]))
        copies[-1].start()
    band_z, band_y = bands(size_y, size_z)
    added = injection(0, cells, traces, size_z)
    for b in range(blocks):
        inject = added(b * ROWS).reshape(layers, size_y, size_z)
        for i, value in enumerate(laplace_block(now, b * layers, layers, band_z, band_y)):
            x = b * layers + i
            lap[x] = value
            base[x] = 2.0 * now[x] + inject[i]
    for b in range(blocks):
        copies[b].wait()
        part = slice(b * layers, (b + 1) * layers)
        base[part] = base[part] - prev[part]


def later_step(step, flags, *refs):
    y_odd, x_odd, y_even, x_even, base_in, lap_in, prev, courant, forward, cells, traces, *refs = refs
    gradient_in = refs.pop(0) if step > 1 else None
    last = step == STEPS - 1
    now, lap, gradient = refs[:3]
    base = None if last else refs[3]
    size_x, size_y, size_z = now.shape
    layers = ROWS // size_y
    band_z, band_y = bands(size_y, size_z)
    x_change = x_changes(flags, x_even, x_odd, size_x)
    for x in range(size_x):
        value = with_change(lap_in[x], x, x_change, y_tiles(flags, y_even, y_odd, x))
        now[x] = base_in[x] + (courant[x] * TWELFTH) * value
        value = forward[step - 1, x].astype(jnp.float32) * value
        gradient[x] = gradient_in[x] + value if step > 1 else value
    added = None if last else injection(step, cells, traces, size_z)
    for b in range(size_x // layers):
        inject = None if last else added(b * ROWS).reshape(layers, size_y, size_z)
        for i, value in enumerate(laplace_block(now, b * layers, layers, band_z, band_y)):
            x = b * layers + i
            lap[x] = value
            if last:
                gradient[x] += forward[step, x].astype(jnp.float32) * value
            else:
                base[x] = (2.0 * now[x] - prev[x]) + inject[i]


def finish(flags, y_odd, x_odd, y_even, x_even, now, lap, prev, courant, cells, traces, next_hbm, now_hbm, nxt, sems):
    size_x, size_y, size_z = now.shape
    layers = ROWS // size_y
    keep = pltpu.make_async_copy(now, now_hbm, sems.at[0])
    keep.start()
    added = injection(STEPS - 1, cells, traces, size_z)
    x_change = x_changes(flags, x_even, x_odd, size_x)
    copies = []
    for b in range(size_x // layers):
        inject = added(b * ROWS).reshape(layers, size_y, size_z)
        for i in range(layers):
            x = b * layers + i
            value = with_change(lap[x], x, x_change, y_tiles(flags, y_even, y_odd, x))
            base = (2.0 * now[x] - prev[x]) + inject[i]
            nxt[x] = base + (courant[x] * TWELFTH) * value
        part = pl.ds(b * layers, layers)
        copies.append(pltpu.make_async_copy(nxt.at[part], next_hbm.at[part], sems.at[1 + b]))
        copies[-1].start()
    for copy in copies:
        copy.wait()
    keep.wait()


def project_z(flags, y_odd, x_odd, y_even, x_even, forward, gradient, table_z, coef):
    size_x, size_y, _ = gradient.shape
    table = split(table_z[...])
    x_change = x_changes(flags, x_even, x_odd, size_x)
    for s in range(8):
        lines = []
        for x in range(4 * s, 4 * s + 4):
            first, last = y_tiles(flags, y_even, y_odd, x)
            scale = forward[STEPS - 1, x].astype(jnp.float32)
            tiles = (scale[0:8] * first, scale[size_y - 8 : size_y] * last)
            value = with_change(gradient[x], x, {}, tiles)
            lines.append(value + scale * x_change[x] if x in x_change else value)
        value = dot3(table, split(jnp.concatenate(lines, axis=0)), NT)
        coef[pl.ds(s, value.shape[0], stride=8), :] = value


def project_y(chunks, table_y, out, plane):
    count = chunks.shape[0] // GROUP
    for r in range(GROUP):
        for q in range(4):
            pieces = [chunks[r * count + c][:, q * 32 : (q + 1) * 32] for c in range(count)]
            plane[pl.ds((r * 4 + q) * 8, 8), :] = jnp.concatenate(pieces, axis=1)
    out[...] = dot3(split(plane[...]), split(table_y[...]), NT)


def smooth_plane(flags, own, one, two, three, table_x, table_y, chunks, plane):
    high, low = split(jnp.concatenate([own[...], one[...], two[...], three[...]], axis=0))
    tables = [split(table_x[flags[6 + k]]) for k in range(GROUP)]
    left_high = jnp.concatenate([table[0] for table in tables], axis=1)
    left_low = jnp.concatenate([table[1] for table in tables], axis=1)
    total = dot3((left_high, left_low), (high, low), NN)
    plane[...] = dot3(split(total), split(table_y[...]), NN)
    count = chunks.shape[0] // GROUP
    for r in range(GROUP):
        for c in range(count):
            pieces = [plane[pl.ds((r * 4 + q) * 8, 8), c * 32 : (c + 1) * 32] for q in range(4)]
            chunks[r * count + c] = jnp.concatenate(pieces, axis=1)


def expand_z(coef, table_z, out, lines, sems):
    _, size_y, size_z = out.shape
    high, low = split(table_z[...])
    table = jnp.concatenate([high, high, low], axis=0)
    copies = []
    for s in range(8):
        high, low = split(coef[pl.ds(s, coef.shape[0] // 8, stride=8), :])
        value = dot(jnp.concatenate([high, low, high], axis=0), table, TN)
        lines[s] = value.reshape(4, size_y, size_z)
        copies.append(pltpu.make_async_copy(lines.at[s], out.at[pl.ds(4 * s, 4)], sems.at[s]))
        copies[-1].start()
    for copy in copies:
        copy.wait()


def call(kernel, out_shape, specs, out_specs=None, scratch=(), room=24, **cost):
    return pl.pallas_call(
        kernel,
        out_shape=out_shape,
        in_specs=specs,
        out_specs=out_specs or jax.tree.map(lambda _: VMEM, out_shape),
        scratch_shapes=scratch,
        compiler_params=pltpu.CompilerParams(vmem_limit_bytes=int(room * 2**20)),
        cost_estimate=pl.CostEstimate(transcendentals=0, **cost),
    )


def per_device(forward_fields, adjoint_now, adjoint_prev, courant_sq, receiver_cells, traces):
    shape = adjoint_now.shape
    size_x, size_y, size_z = shape
    rows, cols = lax.axis_size("row"), lax.axis_size("col")
    both = ("row", "col")
    spot = lax.axis_index(both).reshape(1)
    placed = functools.partial(functools.partial, with_flags, rows, cols)
    basis_z = basis(KZ, size_z)
    table_z = jnp.asarray(basis_z, jnp.float32)
    table_z_scaled = jnp.asarray(basis_z * TWELFTH, jnp.float32)
    table_y = jnp.asarray(basis(KY, cols * size_y), jnp.float32)
    basis_x = basis(KX, rows * size_x)
    low_pass = (basis_x.T @ basis_x)[0]
    span = rows // GROUP
    own = span * size_x
    cells = (np.arange(4)[:, None] + 4 * np.arange(8)[None, :]).reshape(-1)
    place = (np.arange(span)[:, None] * GROUP * size_x + cells[None, :]).reshape(-1)
    gap = place[:, None] - place[None, :]
    table_x = jnp.asarray(
        np.stack([low_pass[(gap + k * size_x) % low_pass.size] for k in range(1 - GROUP, GROUP)]),
        jnp.float32,
    )

    field = jax.ShapeDtypeStruct(shape, jnp.float32)
    x_face = jax.ShapeDtypeStruct((2, size_y, size_z), jnp.float32)
    y_face = jax.ShapeDtypeStruct((size_x, 2, size_z), jnp.float32)
    chunks = jax.ShapeDtypeStruct((KZ, 8, 128), jnp.float32)
    lines = jax.ShapeDtypeStruct((KZ * 8, 128), jnp.float32)
    swaps = [[], [], [], []]
    for r in range(rows):
        for c in range(cols):
            up, right = r + 2 * (r % 2) - 1, c + 2 * (c % 2) - 1
            targets = (
                (r ^ 1, c),
                (up, c) if 0 <= up < rows else (r, c ^ 1),
                (r, c ^ 1),
                (r, right) if 0 <= right < cols else (r ^ 1, c),
            )
            for pairs, (to_row, to_col) in zip(swaps, targets):
                pairs.append((r * cols + c, to_row * cols + to_col))
    heavy = dict(flops=2 * 10**9, bytes_accessed=7 * 2**20)
    light = dict(flops=10**6, bytes_accessed=2**18)
    whole = pltpu.VMEM(shape, jnp.float32)
    blocks = size_x * size_y // ROWS

    now, *faces = call(
        placed(pack),
        (field, y_face, x_face, y_face, x_face),
        [SMEM, HBM],
        scratch=[DMA((4,))],
        room=PACK_ROOM,
        **light,
    )(spot, adjoint_now)
    spots, values = receiver_cells, traces
    halo = gradient = prev = None
    for step in range(STEPS):
        sent = [lax.ppermute(face, both, swaps[i]) for i, face in zip(ORDER, faces)]
        if step == 0:
            base, lap = call(
                first_step,
                (field, field),
                [VMEM, HBM, VMEM, VMEM],
                scratch=[whole, DMA((blocks,))],
                room=FIRST_ROOM,
                **heavy,
            )(now, adjoint_prev, spots, values)
        else:
            last = step == STEPS - 1
            operands = (spot, *halo, base, lap, now, courant_sq, forward_fields, spots, values)
            if step > 1:
                operands += (gradient,)
            prev = now
            results = call(
                placed(functools.partial(later_step, step)),
                (field,) * (3 if last else 4),
                [SMEM] + [VMEM] * (len(operands) - 1),
                **heavy,
            )(*operands)
            now, lap, gradient = results[:3]
            base = None if last else results[3]
        halo = sent
        if step < STEPS - 1:
            faces = call(
                placed(faces_after), (y_face, x_face, y_face, x_face), [SMEM] + [VMEM] * 7, **light
            )(spot, *halo, courant_sq, base, lap)
    coef = call(placed(project_z), lines, [SMEM] + [VMEM] * 7, **light)(
        spot, *halo, forward_fields, gradient, table_z_scaled
    )
    final_now, final_prev = call(
        placed(finish),
        (field, field),
        [SMEM] + [VMEM] * 10,
        out_specs=(HBM, HBM),
        scratch=[whole, DMA((1 + blocks,))],
        **heavy,
    )(spot, *halo, now, lap, prev, courant_sq, spots, values)

    groups = [
        [(m * GROUP + g) * cols + c for m in range(span) for c in range(cols)] for g in range(GROUP)
    ]
    coef = coef.reshape(chunks.shape)
    coef = lax.all_to_all(coef, both, 0, 0, axis_index_groups=groups, tiled=True)
    plane = jax.ShapeDtypeStruct((own, KY), jnp.float32)
    wide = pltpu.VMEM((own, cols * size_y), jnp.float32)
    mine = call(project_y, plane, [VMEM] * 2, scratch=[wide], **light)(coef, table_y)
    beside, across = ([(i, i ^ k) for i in range(rows)] for k in (1, 2))
    two = lax.ppermute(mine, "row", across)
    one = lax.ppermute(mine, "row", beside)
    two, final_now, final_prev = lax.optimization_barrier((two, final_now, final_prev))
    others = (one, two, lax.ppermute(two, "row", beside))
    coef = call(
        placed(smooth_plane),
        chunks,
        [SMEM] + [VMEM] * 6,
        scratch=[wide],
        **light,
    )(
        spot, mine, *others, table_x, table_y
    )
    coef = lax.all_to_all(coef, both, 0, 0, axis_index_groups=groups, tiled=True)
    smoothed = call(
        expand_z,
        field,
        [VMEM] * 2,
        out_specs=HBM,
        scratch=[pltpu.VMEM((8, 4, size_y, size_z), jnp.float32), DMA((8,))],
        **light,
    )(coef.reshape(lines.shape), table_z)
    return (smoothed, final_now, final_prev)


def solution(mesh):
    in_specs = (
        P(None, "row", "col", None),
        P("row", "col", None),
        P("row", "col", None),
        P("row", "col", None),
        P("row", "col", None),
        P("row", "col", None, None),
    )
    out_specs = (P("row", "col", None), P("row", "col", None), P("row", "col", None))
    return jax.shard_map(
        per_device, mesh=mesh, in_specs=in_specs, out_specs=out_specs, check_vma=False
    )
```

```python
import functools

import jax
import jax.numpy as jnp
import numpy as np
from jax import lax
from jax.experimental import pallas as pl
from jax.experimental.pallas import tpu as pltpu
from jax.sharding import PartitionSpec as P

STEPS = 4
KX = 128
KY = 128
KZ = 64
GROUP = 4
ROWS = 256
TWELFTH = 1.0 / 12.0
PACK_ROOM = 52
FIRST_ROOM = 50
ORDER = (3, 2, 1, 0)

HBM = pl.BlockSpec(memory_space=pltpu.HBM)
VMEM = pl.BlockSpec(memory_space=pltpu.VMEM)
SMEM = pl.BlockSpec(memory_space=pltpu.SMEM)
DMA = pltpu.SemaphoreType.DMA
NT = (((1,), (1,)), ((), ()))
NN = (((1,), (0,)), ((), ()))
TN = (((0,), (0,)), ((), ()))


def split(value):
    high = value.astype(jnp.bfloat16)
    low = (value - high.astype(jnp.float32)).astype(jnp.bfloat16)
    return high, low


def dot(left, right, dims):
    return lax.dot_general(left, right, dims, preferred_element_type=jnp.float32)


def dot3(left, right, dims):
    return (
        dot(left[0], right[0], dims)
        + dot(left[1], right[0], dims)
        + dot(left[0], right[1], dims)
    )


def basis(count, length):
    half = count // 2
    cells = np.arange(length, dtype=np.int64)[None, :]
    modes = np.arange(count, dtype=np.int64)[:, None]
    freq = np.where(modes < half, modes, modes - half + 1)
    phase = (freq * cells % length) * (2.0 * np.pi / length)
    values = np.sqrt(2.0 / length) * np.where(modes < half, np.cos(phase), np.sin(phase))
    values[0] = np.sqrt(1.0 / length)
    values[count - 1] = 0.0
    return values


def bands(size_y, size_z):
    def far(size):
        one = lax.broadcasted_iota(jnp.int32, (size, size), 0)
        two = lax.broadcasted_iota(jnp.int32, (size, size), 1)
        return jnp.abs(one - two), one // size_y == two // size_y

    gap, _ = far(size_z)
    band_z = jnp.where(gap == 0, -90.0, jnp.where(gap == 1, 16.0, jnp.where(gap == 2, -1.0, 0.0)))
    gap, same = far(ROWS)
    band_y = jnp.where(gap == 1, 16.0, jnp.where(gap == 2, -1.0, 0.0))
    band_y = jnp.where(same, band_y, 0.0)
    return band_z.astype(jnp.bfloat16), band_y.astype(jnp.bfloat16)


def with_flags(rows, cols, kernel, spot, *refs):
    row, col = spot[0] >> (cols.bit_length() - 1), spot[0] & (cols - 1)
    turn = row & (GROUP - 1)
    flags = [row, rows - 1 - row, col, cols - 1 - col, row & 1, col & 1]
    flags += [turn - (turn ^ k) + GROUP - 1 for k in range(GROUP)]
    kernel(flags, *refs)


def pack(flags, now_hbm, now, y_odd, y_even, x_odd, x_even, sems):
    size_x, size_y, _ = now.shape
    step = size_x // 4
    copies = []
    for b in range(4):
        part = pl.ds(b * step, step)
        copies.append(pltpu.make_async_copy(now_hbm.at[part], now.at[part], sems.at[b]))
        copies[-1].start()
    for b in range(4):
        copies[b].wait()
        part = pl.ds(b * step, step)
        low, high = now[part, 0:2, :], now[part, size_y - 2 : size_y, :]
        y_even[part] = jnp.where(flags[5] > 0, low, high)
        y_odd[part] = jnp.where(flags[5] > 0, high, low)
    low, high = now[0:2], now[size_x - 2 : size_x]
    x_even[...] = jnp.where(flags[4] > 0, low, high)
    x_odd[...] = jnp.where(flags[4] > 0, high, low)


def x_changes(flags, x_even, x_odd, size_x):
    odd = flags[4] > 0
    before = [jnp.where(odd, x_even[i], x_odd[i]) for i in range(2)]
    after = [jnp.where(odd, x_odd[i], x_even[i]) for i in range(2)]
    before = [jnp.where(flags[0] > 0, value, 0.0) for value in before]
    after = [jnp.where(flags[1] > 0, value, 0.0) for value in after]
    return {
        0: 16.0 * before[1] - before[0],
        1: -before[1],
        size_x - 2: -after[0],
        size_x - 1: 16.0 * after[0] - after[1],
    }


def y_tiles(flags, y_even, y_odd, x):
    size_z = y_even.shape[2]
    line = lax.broadcasted_iota(jnp.int32, (8, size_z), 0)
    odd = flags[5] > 0
    low = jnp.where(flags[2] > 0, jnp.where(odd, y_even[x], y_odd[x]), 0.0)
    near = jnp.broadcast_to(low[1:2], (8, size_z))
    far = jnp.broadcast_to(low[0:1], (8, size_z))
    first = jnp.where(line == 0, 16.0 * near - far, jnp.where(line == 1, -near, 0.0))
    high = jnp.where(flags[3] > 0, jnp.where(odd, y_odd[x], y_even[x]), 0.0)
    near = jnp.broadcast_to(high[0:1], (8, size_z))
    far = jnp.broadcast_to(high[1:2], (8, size_z))
    last = jnp.where(line == 7, 16.0 * near - far, jnp.where(line == 6, -near, 0.0))
    return first, last


def with_change(value, x, x_change, tiles):
    size_y = value.shape[0]
    parts = [value[0:8] + tiles[0], value[8 : size_y - 8], value[size_y - 8 : size_y] + tiles[1]]
    value = jnp.concatenate(parts, axis=0)
    return value + x_change[x] if x in x_change else value


def faces_after(flags, y_odd, y_even, x_odd, x_even, courant, base, lap, out_y_odd, out_y_even, out_x_odd, out_x_even):
    size_x, size_y, _ = base.shape
    x_change = x_changes(flags, x_even, x_odd, size_x)
    layers = {}
    for x in range(size_x):
        tiles = y_tiles(flags, y_even, y_odd, x)
        if x in x_change:
            value = with_change(lap[x], x, x_change, tiles)
            layers[x] = value = base[x] + (courant[x] * TWELFTH) * value
            first, last = value[0:8], value[size_y - 8 : size_y]
        else:
            first = base[x, 0:8] + (courant[x, 0:8] * TWELFTH) * (lap[x, 0:8] + tiles[0])
            end = slice(size_y - 8, size_y)
            last = base[x, end] + (courant[x, end] * TWELFTH) * (lap[x, end] + tiles[1])
        low, high = first[0:2], last[6:8]
        out_y_even[x] = jnp.where(flags[5] > 0, low, high)
        out_y_odd[x] = jnp.where(flags[5] > 0, high, low)
    for i in range(2):
        low, high = layers[i], layers[size_x - 2 + i]
        out_x_even[i] = jnp.where(flags[4] > 0, low, high)
        out_x_odd[i] = jnp.where(flags[4] > 0, high, low)


def injection(step, cells, traces, size_z):
    spots = cells[0]
    value = traces[0, 0, pl.ds(step, 1), :]
    top = value.astype(jnp.bfloat16)
    rest = value - top.astype(jnp.float32)
    mid = rest.astype(jnp.bfloat16)
    depth = lax.broadcasted_iota(jnp.int32, (size_z, spots.shape[1]), 0)
    here = depth == spots % size_z
    parts = [
        jnp.where(here, part.astype(jnp.float32), 0.0).astype(jnp.bfloat16)
        for part in (top, mid)
    ]
    line = lax.broadcasted_iota(jnp.int32, (ROWS, spots.shape[1]), 0)

    def block(first_row):
        hits = jnp.where(line == spots // size_z - first_row, 1.0, 0.0).astype(jnp.bfloat16)
        return sum(dot(hits, part, NT) for part in parts)

    return block


def laplace_block(now, first, layers, band_z, band_y):
    size_x, size_y, size_z = now.shape
    center = now[first : first + layers].reshape(ROWS, size_z)
    high, low = split(center)
    lap = dot(high, band_z, NN) + dot(low, band_z, NN)
    lap = lap + dot(band_y, high, NN) + dot(band_y, low, NN)
    lap = lap.reshape(layers, size_y, size_z)
    out = []
    for layer in range(layers):
        x = first + layer
        near = [now[x + d] for d in (-1, 1) if 0 <= x + d < size_x]
        far = [now[x + d] for d in (-2, 2) if 0 <= x + d < size_x]
        value = lap[layer] + 16.0 * functools.reduce(jnp.add, near)
        out.append(value - functools.reduce(jnp.add, far))
    return out


def first_step(now, prev_hbm, cells, traces, base, lap, prev, sems):
    size_x, size_y, size_z = now.shape
    layers = ROWS // size_y
    blocks = size_x // layers
    copies = []
    for b in range(blocks):
        part = pl.ds(b * layers, layers)
        copies.append(pltpu.make_async_copy(prev_hbm.at[part], prev.at[part], sems.at[b]))
        copies[-1].start()
    band_z, band_y = bands(size_y, size_z)
    added = injection(0, cells, traces, size_z)
    for b in range(blocks):
        inject = added(b * ROWS).reshape(layers, size_y, size_z)
        for i, value in enumerate(laplace_block(now, b * layers, layers, band_z, band_y)):
            x = b * layers + i
            lap[x] = value
            base[x] = 2.0 * now[x] + inject[i]
    for b in range(blocks):
        copies[b].wait()
        part = slice(b * layers, (b + 1) * layers)
        base[part] = base[part] - prev[part]


def later_step(step, flags, *refs):
    y_odd, y_even, x_odd, x_even, base_in, lap_in, prev, courant, forward, cells, traces, *refs = refs
    gradient_in = refs.pop(0) if step > 1 else None
    last = step == STEPS - 1
    now, lap, gradient = refs[:3]
    base = None if last else refs[3]
    size_x, size_y, size_z = now.shape
    layers = ROWS // size_y
    band_z, band_y = bands(size_y, size_z)
    x_change = x_changes(flags, x_even, x_odd, size_x)
    for x in range(size_x):
        value = with_change(lap_in[x], x, x_change, y_tiles(flags, y_even, y_odd, x))
        now[x] = base_in[x] + (courant[x] * TWELFTH) * value
        value = forward[step - 1, x].astype(jnp.float32) * value
        gradient[x] = gradient_in[x] + value if step > 1 else value
    added = None if last else injection(step, cells, traces, size_z)
    for b in range(size_x // layers):
        inject = None if last else added(b * ROWS).reshape(layers, size_y, size_z)
        for i, value in enumerate(laplace_block(now, b * layers, layers, band_z, band_y)):
            x = b * layers + i
            lap[x] = value
            if last:
                gradient[x] += forward[step, x].astype(jnp.float32) * value
            else:
                base[x] = (2.0 * now[x] - prev[x]) + inject[i]


def finish(flags, y_odd, y_even, x_odd, x_even, now, lap, prev, courant, cells, traces, next_hbm, now_hbm, nxt, sems):
    size_x, size_y, size_z = now.shape
    layers = ROWS // size_y
    keep = pltpu.make_async_copy(now, now_hbm, sems.at[0])
    keep.start()
    added = injection(STEPS - 1, cells, traces, size_z)
    x_change = x_changes(flags, x_even, x_odd, size_x)
    copies = []
    for b in range(size_x // layers):
        inject = added(b * ROWS).reshape(layers, size_y, size_z)
        for i in range(layers):
            x = b * layers + i
            value = with_change(lap[x], x, x_change, y_tiles(flags, y_even, y_odd, x))
            base = (2.0 * now[x] - prev[x]) + inject[i]
            nxt[x] = base + (courant[x] * TWELFTH) * value
        part = pl.ds(b * layers, layers)
        copies.append(pltpu.make_async_copy(nxt.at[part], next_hbm.at[part], sems.at[1 + b]))
        copies[-1].start()
    for copy in copies:
        copy.wait()
    keep.wait()


def project_z(flags, y_odd, y_even, x_odd, x_even, forward, gradient, table_z, coef):
    size_x, size_y, _ = gradient.shape
    table = split(table_z[...])
    x_change = x_changes(flags, x_even, x_odd, size_x)
    for s in range(8):
        lines = []
        for x in range(4 * s, 4 * s + 4):
            first, last = y_tiles(flags, y_even, y_odd, x)
            scale = forward[STEPS - 1, x].astype(jnp.float32)
            tiles = (scale[0:8] * first, scale[size_y - 8 : size_y] * last)
            value = with_change(gradient[x], x, {}, tiles)
            lines.append(value + scale * x_change[x] if x in x_change else value)
        value = dot3(table, split(jnp.concatenate(lines, axis=0)), NT)
        coef[pl.ds(s, value.shape[0], stride=8), :] = value


def project_y(chunks, table_y, out, plane):
    count = chunks.shape[0] // GROUP
    for r in range(GROUP):
        for q in range(4):
            pieces = [chunks[r * count + c][:, q * 32 : (q + 1) * 32] for c in range(count)]
            plane[pl.ds((r * 4 + q) * 8, 8), :] = jnp.concatenate(pieces, axis=1)
    out[...] = dot3(split(plane[...]), split(table_y[...]), NT)


def smooth_plane(flags, own, one, two, three, table_x, table_y, chunks, plane):
    high, low = split(jnp.concatenate([own[...], one[...], two[...], three[...]], axis=0))
    tables = [split(table_x[flags[6 + k]]) for k in range(GROUP)]
    left_high = jnp.concatenate([table[0] for table in tables], axis=1)
    left_low = jnp.concatenate([table[1] for table in tables], axis=1)
    total = dot3((left_high, left_low), (high, low), NN)
    plane[...] = dot3(split(total), split(table_y[...]), NN)
    count = chunks.shape[0] // GROUP
    for r in range(GROUP):
        for c in range(count):
            pieces = [plane[pl.ds((r * 4 + q) * 8, 8), c * 32 : (c + 1) * 32] for q in range(4)]
            chunks[r * count + c] = jnp.concatenate(pieces, axis=1)


def expand_z(coef, table_z, out, lines, sems):
    _, size_y, size_z = out.shape
    high, low = split(table_z[...])
    table = jnp.concatenate([high, high, low], axis=0)
    copies = []
    for s in range(8):
        high, low = split(coef[pl.ds(s, coef.shape[0] // 8, stride=8), :])
        value = dot(jnp.concatenate([high, low, high], axis=0), table, TN)
        lines[s] = value.reshape(4, size_y, size_z)
        copies.append(pltpu.make_async_copy(lines.at[s], out.at[pl.ds(4 * s, 4)], sems.at[s]))
        copies[-1].start()
    for copy in copies:
        copy.wait()


def call(kernel, out_shape, specs, out_specs=None, scratch=(), room=24, **cost):
    return pl.pallas_call(
        kernel,
        out_shape=out_shape,
        in_specs=specs,
        out_specs=out_specs or jax.tree.map(lambda _: VMEM, out_shape),
        scratch_shapes=scratch,
        compiler_params=pltpu.CompilerParams(vmem_limit_bytes=int(room * 2**20)),
        cost_estimate=pl.CostEstimate(transcendentals=0, **cost),
    )


def per_device(forward_fields, adjoint_now, adjoint_prev, courant_sq, receiver_cells, traces):
    shape = adjoint_now.shape
    size_x, size_y, size_z = shape
    rows, cols = lax.axis_size("row"), lax.axis_size("col")
    both = ("row", "col")
    spot = lax.axis_index(both).reshape(1)
    placed = functools.partial(functools.partial, with_flags, rows, cols)
    basis_z = basis(KZ, size_z)
    table_z = jnp.asarray(basis_z, jnp.float32)
    table_z_scaled = jnp.asarray(basis_z * TWELFTH, jnp.float32)
    table_y = jnp.asarray(basis(KY, cols * size_y), jnp.float32)
    basis_x = basis(KX, rows * size_x)
    low_pass = (basis_x.T @ basis_x)[0]
    span = rows // GROUP
    own = span * size_x
    cells = (np.arange(4)[:, None] + 4 * np.arange(8)[None, :]).reshape(-1)
    place = (np.arange(span)[:, None] * GROUP * size_x + cells[None, :]).reshape(-1)
    gap = place[:, None] - place[None, :]
    table_x = jnp.asarray(
        np.stack([low_pass[(gap + k * size_x) % low_pass.size] for k in range(1 - GROUP, GROUP)]),
        jnp.float32,
    )

    field = jax.ShapeDtypeStruct(shape, jnp.float32)
    x_face = jax.ShapeDtypeStruct((2, size_y, size_z), jnp.float32)
    y_face = jax.ShapeDtypeStruct((size_x, 2, size_z), jnp.float32)
    chunks = jax.ShapeDtypeStruct((KZ, 8, 128), jnp.float32)
    lines = jax.ShapeDtypeStruct((KZ * 8, 128), jnp.float32)
    swaps = [[], [], [], []]
    for r in range(rows):
        for c in range(cols):
            up, right = r + 2 * (r % 2) - 1, c + 2 * (c % 2) - 1
            targets = (
                (r ^ 1, c),
                (up, c) if 0 <= up < rows else (r, c ^ 1),
                (r, c ^ 1),
                (r, right) if 0 <= right < cols else (r ^ 1, c),
            )
            for pairs, (to_row, to_col) in zip(swaps, targets):
                pairs.append((r * cols + c, to_row * cols + to_col))
    heavy = dict(flops=2 * 10**9, bytes_accessed=7 * 2**20)
    light = dict(flops=10**6, bytes_accessed=2**18)
    whole = pltpu.VMEM(shape, jnp.float32)
    blocks = size_x * size_y // ROWS

    now, *faces = call(
        placed(pack),
        (field, y_face, y_face, x_face, x_face),
        [SMEM, HBM],
        scratch=[DMA((4,))],
        room=PACK_ROOM,
        **light,
    )(spot, adjoint_now)
    spots, values = receiver_cells, traces
    halo = gradient = prev = None
    for step in range(STEPS):
        sent = [lax.ppermute(face, both, swaps[i]) for i, face in zip(ORDER, faces)]
        if step == 0:
            base, lap = call(
                first_step,
                (field, field),
                [VMEM, HBM, VMEM, VMEM],
                scratch=[whole, DMA((blocks,))],
                room=FIRST_ROOM,
                **heavy,
            )(now, adjoint_prev, spots, values)
        else:
            last = step == STEPS - 1
            operands = (spot, *halo, base, lap, now, courant_sq, forward_fields, spots, values)
            if step > 1:
                operands += (gradient,)
            prev = now
            results = call(
                placed(functools.partial(later_step, step)),
                (field,) * (3 if last else 4),
                [SMEM] + [VMEM] * (len(operands) - 1),
                **heavy,
            )(*operands)
            now, lap, gradient = results[:3]
            base = None if last else results[3]
        halo = sent
        if step < STEPS - 1:
            faces = call(
                placed(faces_after), (y_face, y_face, x_face, x_face), [SMEM] + [VMEM] * 7, **light
            )(spot, *halo, courant_sq, base, lap)
    coef = call(placed(project_z), lines, [SMEM] + [VMEM] * 7, **light)(
        spot, *halo, forward_fields, gradient, table_z_scaled
    )
    final_now, final_prev = call(
        placed(finish),
        (field, field),
        [SMEM] + [VMEM] * 10,
        out_specs=(HBM, HBM),
        scratch=[whole, DMA((1 + blocks,))],
        **heavy,
    )(spot, *halo, now, lap, prev, courant_sq, spots, values)

    groups = [
        [(m * GROUP + g) * cols + c for m in range(span) for c in range(cols)] for g in range(GROUP)
    ]
    coef = coef.reshape(chunks.shape)
    coef = lax.all_to_all(coef, both, 0, 0, axis_index_groups=groups, tiled=True)
    plane = jax.ShapeDtypeStruct((own, KY), jnp.float32)
    wide = pltpu.VMEM((own, cols * size_y), jnp.float32)
    mine = call(project_y, plane, [VMEM] * 2, scratch=[wide], **light)(coef, table_y)
    beside, across = ([(i, i ^ k) for i in range(rows)] for k in (1, 2))
    two = lax.ppermute(mine, "row", across)
    one = lax.ppermute(mine, "row", beside)
    two, final_now, final_prev = lax.optimization_barrier((two, final_now, final_prev))
    others = (one, two, lax.ppermute(two, "row", beside))
    coef = call(
        placed(smooth_plane),
        chunks,
        [SMEM] + [VMEM] * 6,
        scratch=[wide],
        **light,
    )(
        spot, mine, *others, table_x, table_y
    )
    coef = lax.all_to_all(coef, both, 0, 0, axis_index_groups=groups, tiled=True)
    smoothed = call(
        expand_z,
        field,
        [VMEM] * 2,
        out_specs=HBM,
        scratch=[pltpu.VMEM((8, 4, size_y, size_z), jnp.float32), DMA((8,))],
        **light,
    )(coef.reshape(lines.shape), table_z)
    return (smoothed, final_now, final_prev)


def solution(mesh):
    in_specs = (
        P(None, "row", "col", None),
        P("row", "col", None),
        P("row", "col", None),
        P("row", "col", None),
        P("row", "col", None),
        P("row", "col", None, None),
    )
    out_specs = (P("row", "col", None), P("row", "col", None), P("row", "col", None))
    return jax.shard_map(
        per_device, mesh=mesh, in_specs=in_specs, out_specs=out_specs, check_vma=False
    )
```
